256 devices in a mesh: domain: 32 (over z_hi, x, y), band: 8 (over z_lo, core).
Axes of the slice: x: 4, y: 4, z: 8 (z_hi: 2, z_lo: 4; z = z_hi * 4 + z_lo), core: 2. Of those that a mesh axis runs over, the one named last changes fastest.
Arguments:
- orbitals: float32 [128, 128, 64, 128], P('band', 'domain'), may hold values from -8 to 8, as said below
- potential: float32 [128, 64, 128], P('domain'), may hold values from 0 to 1
Outputs:
- rotated: float32 [128, 128, 64, 128], P(None, 'domain', 'band')
The draws below stay inside these ranges and needn't reach their ends.
Inputs may be any that keep to these rules, and one draw needn't show every extreme that they name: `orbitals`: entries of order one.
All inputs are finite; a program needn't handle non-finite values.
Results may differ from the reference program's by a relative error of at most 0.00015.
Values sent between devices are 32-bit elements; how exact they have to be, the bound alone decides.
No kernel may reach another device: no remote copies, remote signals or barrier semaphores. Data moves between devices by JAX's collectives and lax.ppermute only.
A program may use at most 128 MiB of HBM per device.

```python
import math
import jax
import jax.numpy as jnp
from jax import lax

ORB = 128
NX = 128
NY = 64
NZ = 128


def draw_orbitals(key, part):
    first_key = jax.random.fold_in(key, 11)
    plane = jnp.arange(NZ, dtype=jnp.float32)
    ramp = (1.0 + 0.75 * plane / (NZ - 1.0)).reshape(1, NZ, 1, 1)
    values = jnp.clip(jax.random.normal(first_key, (ORB, NZ, NY, NX), jnp.float32), -4.5, 4.5)
    return (values * ramp).astype(jnp.float32)


def shard_levels(key, shape, cuts, least, top_value):
    level, own = 1.0, jax.random.fold_in(key, 6)
    for position, shards_of in cuts:
        steps = jnp.exp(jax.random.uniform(jax.random.fold_in(own, position), (shards_of,), jnp.float32, least / len(cuts), top_value / len(cuts)))
        level = level * jnp.repeat(steps, shape[position] // shards_of).reshape([-1 if axis == position else 1 for axis in range(len(shape))])
    return level


def setup_inputs(seed: int = 0) -> dict:
    splits = jax.random.split(jax.random.key(seed), 3)
    return {
        "orbitals": draw_orbitals(jax.random.fold_in(splits[2], 71), 0),
        "potential": jnp.clip(1.0 * jax.random.uniform(splits[1], (NZ, NY, NX), jnp.float32) ** shard_levels(splits[1], (NZ, NY, NX), ((0, 32),), -0.2, 0.2), 0.0, 1.0),
    }


def apply_shift(field, potential):
    padded = jnp.pad(field, ((0, 0), (1, 1), (0, 0), (0, 0)), mode='wrap')
    middle = padded[:, 1:-1]
    beside = padded[:, 2:] + padded[:, :-2]
    beside = beside + jnp.roll(middle, 1, 2) + jnp.roll(middle, -1, 2)
    beside = beside + jnp.roll(middle, 1, 3) + jnp.roll(middle, -1, 3)
    hamil = (3.0 + potential[None]) * middle - 0.5 * beside
    return (hamil - 4.5 * middle) / 2.5

def reference(orbitals, potential):
    first = apply_shift(orbitals, potential)
    second = 2.0 * apply_shift(first, potential) - orbitals
    filtered = 2.0 * apply_shift(second, potential) - first
    flat = filtered.reshape(ORB, -1)
    gram = jnp.dot(flat.astype(jnp.float32), flat.T.astype(jnp.float32), precision=lax.Precision.HIGHEST, preferred_element_type=jnp.float32)
    lower = jnp.linalg.cholesky(gram)
    solved = lax.linalg.triangular_solve(lower, flat, left_side=True, lower=True)
    scaled = solved * math.sqrt(NX * NY * NZ)
    return scaled.reshape(ORB, NZ, NY, NX).astype(jnp.float32)
```

```python
import functools
import math

import jax
import jax.numpy as jnp
from jax import lax
from jax.experimental import pallas as pl
from jax.experimental.pallas import tpu as pltpu
from jax.sharding import PartitionSpec as P

DEPTH = 3
PARTS = 1


def permuted(block, axis, target):
    count = lax.axis_size(axis)
    return lax.ppermute(block, axis, [(i, target(i)) for i in range(count)])


def neighbours(plane):
    rows, lanes = plane.shape
    beside = pltpu.roll(plane, 1, 0) + pltpu.roll(plane, rows - 1, 0)
    return beside + pltpu.roll(plane, 1, 1) + pltpu.roll(plane, lanes - 1, 1)


def filter_kernel(planes, stripes, field, low, high, pot, pot_low, pot_high, *rest):
    outs, (one, two, three) = rest[:stripes], rest[stripes:]
    me = lax.axis_index("band")

    def source(k):
        if k < DEPTH:
            return low[0, k], pot_low[k]
        if k < DEPTH + planes:
            return field[0, k - DEPTH], pot[k - DEPTH]
        return high[0, k - DEPTH - planes], pot_high[k - DEPTH - planes]

    top = planes + 2 * DEPTH
    for k in range(1, top - 1):
        middle, local = source(k)
        beside = source(k - 1)[0] + source(k + 1)[0] + neighbours(middle)
        one[k] = (0.4 * local - 0.6) * middle - 0.2 * beside
    for k in range(2, top - 2):
        middle = one[k]
        beside = one[k - 1] + one[k + 1] + neighbours(middle)
        before, local = source(k)
        two[k] = (0.8 * local - 1.2) * middle - 0.4 * beside - before
    for k in range(3, top - 3):
        middle = two[k]
        beside = two[k - 1] + two[k + 1] + neighbours(middle)
        _, local = source(k)
        three[k - 3] = (0.8 * local - 1.2) * middle - 0.4 * beside - one[k]
    width = outs[0].shape[2]
    for slot in range(stripes):
        start = pl.multiple_of(jnp.bitwise_xor(me, slot) * width, width)
        outs[slot][0] = three[:, pl.ds(start, width), :]


def filtered_stripes(field, low, high, pot, pot_low, pot_high, stripes):
    count, planes, rows, lanes = field.shape
    width = rows // stripes
    top = planes + 2 * DEPTH

    def by_orbital(depth):
        return pl.BlockSpec((1, depth, rows, lanes), lambda i: (i, 0, 0, 0))

    def whole(depth):
        return pl.BlockSpec((depth, rows, lanes), lambda i: (0, 0, 0))

    out_spec = pl.BlockSpec((1, planes, width, lanes), lambda i: (i, 0, 0, 0))
    shape = jax.ShapeDtypeStruct((count, planes, width, lanes), jnp.float32)
    return pl.pallas_call(
        functools.partial(filter_kernel, planes, stripes),
        grid=(count,),
        in_specs=[by_orbital(planes), by_orbital(DEPTH), by_orbital(DEPTH)]
        + [whole(planes), whole(DEPTH), whole(DEPTH)],
        out_specs=[out_spec] * stripes,
        out_shape=[shape] * stripes,
        scratch_shapes=[
            pltpu.VMEM((top, rows, lanes), jnp.float32),
            pltpu.VMEM((top, rows, lanes), jnp.float32),
            pltpu.VMEM((planes, rows, lanes), jnp.float32),
        ],
        compiler_params=pltpu.CompilerParams(vmem_limit_bytes=32 * 1024 * 1024),
    )(field, low, high, pot, pot_low, pot_high)


def gram_kernel(pieces, cells, *rest):
    refs, (flat, gram) = rest[:-2], rest[-2:]
    me = lax.axis_index("band")
    lanes = refs[0].shape[1]
    share = refs[0].shape[0] // cells
    for index, ref in enumerate(refs):
        slot, piece = divmod(index, pieces)
        first = jnp.bitwise_xor(me, slot) * (share * pieces) + piece * share
        rows = pl.ds(pl.multiple_of(first, share), share)
        for r in range(cells):
            flat[rows, r * lanes : (r + 1) * lanes] = ref[pl.ds(r, share, stride=cells), :]
    whole = flat[...]
    gram[...] = lax.dot_general(
        whole,
        whole,
        (((1,), (1,)), ((), ())),
        precision=lax.Precision.HIGHEST,
        preferred_element_type=jnp.float32,
    )


def flat_and_gram(slots, orbitals):
    pieces = len(slots[0])
    _, planes, width, lanes = slots[0][0].shape
    cells = planes * width
    refs = [piece.reshape(-1, lanes) for slot in slots for piece in slot]
    return pl.pallas_call(
        functools.partial(gram_kernel, pieces, cells),
        out_shape=[
            jax.ShapeDtypeStruct((orbitals, cells * lanes), jnp.float32),
            jax.ShapeDtypeStruct((orbitals, orbitals), jnp.float32),
        ],
        compiler_params=pltpu.CompilerParams(vmem_limit_bytes=32 * 1024 * 1024),
    )(*refs)


def rotate_kernel(cells, inverse, flat, out):
    orbitals = inverse.shape[0]
    lanes = out.shape[1]
    solved = jnp.dot(
        inverse[...],
        flat[...],
        precision=lax.Precision.HIGHEST,
        preferred_element_type=jnp.float32,
    )
    for r in range(cells):
        out[pl.ds(r, orbitals, stride=cells), :] = solved[:, r * lanes : (r + 1) * lanes]


def rotated(inverse, flat, lanes):
    orbitals, columns = flat.shape
    cells = columns // lanes
    return pl.pallas_call(
        functools.partial(rotate_kernel, cells),
        out_shape=jax.ShapeDtypeStruct((orbitals * cells, lanes), jnp.float32),
        compiler_params=pltpu.CompilerParams(vmem_limit_bytes=32 * 1024 * 1024),
    )(inverse, flat)


def summed(gram):
    for bit in (1, 2, 4):
        gram = gram + permuted(gram, "band", lambda i: i ^ bit)
    side = 4
    turned = [
        permuted(gram, "domain", lambda i: i // side * side + (i + k) % side) for k in (1, 2, 3)
    ]
    gram = (gram + turned[0]) + (turned[1] + turned[2])
    plane = side * side
    turned = [
        permuted(gram, "domain", lambda i: i // plane * plane + (i + k * side) % plane)
        for k in (1, 2, 3)
    ]
    gram = (gram + turned[0]) + (turned[1] + turned[2])
    return gram + permuted(gram, "domain", lambda i: i ^ plane)


def body(orbitals, potential):
    domains = lax.axis_size("domain")
    stripes = lax.axis_size("band")
    own, planes, ny_all, nx_all = orbitals.shape
    width = ny_all // stripes
    orb_total = own * stripes
    cell_total = planes * domains * ny_all * nx_all
    up = lambda i: (i + 1) % domains
    down = lambda i: (i - 1) % domains

    pot_low = permuted(potential[planes - DEPTH :], "domain", up)
    pot_high = permuted(potential[:DEPTH], "domain", down)
    share = own // PARTS
    pieces = []
    for part in range(PARTS):
        field = orbitals[part * share : (part + 1) * share]
        low = permuted(field[:, planes - DEPTH :], "domain", up)
        high = permuted(field[:, :DEPTH], "domain", down)
        slots = filtered_stripes(field, low, high, potential, pot_low, pot_high, stripes)
        pieces.append(
            [slots[0]]
            + [permuted(slots[k], "band", lambda i: i ^ k) for k in range(1, stripes)]
        )
    slots = [[piece[k] for piece in pieces] for k in range(stripes)]
    flat, partial_gram = flat_and_gram(slots, orb_total)
    gram = summed(partial_gram)
    lower = jnp.linalg.cholesky(gram)
    inverse = lax.linalg.triangular_solve(
        lower, math.sqrt(cell_total) * jnp.eye(orb_total, dtype=jnp.float32), left_side=True, lower=True
    )
    return rotated(inverse, flat, nx_all).reshape(orb_total, planes, width, nx_all)


def solution(mesh):
    in_specs = (P("band", "domain", None, None), P("domain", None, None))
    out_specs = P(None, "domain", "band", None)
    return jax.shard_map(body, mesh=mesh, in_specs=in_specs, out_specs=out_specs, check_vma=False)
```

```python
import functools
import math

import jax
import jax.numpy as jnp
from jax import lax
from jax.experimental import pallas as pl
from jax.experimental.pallas import tpu as pltpu
from jax.sharding import PartitionSpec as P

DEPTH = 3
PARTS = 1
PANEL = 32
SIDE = 4
SHARES = (6, 4, 3, 3)


def permuted(block, axis, target):
    count = lax.axis_size(axis)
    return lax.ppermute(block, axis, [(i, target(i)) for i in range(count)])


def neighbours(plane):
    rows, lanes = plane.shape
    beside = pltpu.roll(plane, 1, 0) + pltpu.roll(plane, rows - 1, 0)
    return beside + pltpu.roll(plane, 1, 1) + pltpu.roll(plane, lanes - 1, 1)


def filter_kernel(shares, stripes, field, low, high, pot, pot_low, pot_high, pot_seam, *rest):
    routes = len(shares)
    seams, outs = rest[:routes], rest[routes : routes + stripes]
    zero, one, two, three, local = rest[routes + stripes :]
    me = lax.axis_index("band")
    at = lax.rem(lax.axis_index("domain"), SIDE * SIDE)
    at_low, at_high = at == 0, at == SIDE * SIDE - 1
    planes = field.shape[1]
    top = planes + 2 * DEPTH
    width = outs[0].shape[2]
    own = pl.ds(DEPTH, planes)
    local[own] = 0.8 * pot[...] - 1.2
    local[:DEPTH] = 0.8 * jnp.where(at_low, pot_seam[...], pot_low[...]) - 1.2
    local[planes + DEPTH :] = 0.8 * jnp.where(at_high, pot_seam[...], pot_high[...]) - 1.2

    def one_orbital(orbital, seam_plane):
        zero[own] = field[orbital]
        for k in range(DEPTH):
            zero[k] = jnp.where(at_low, seam_plane(k), low[orbital, k])
            zero[planes + DEPTH + k] = jnp.where(at_high, seam_plane(k), high[orbital, k])
        for k in range(1, top - 1):
            beside = zero[k - 1] + zero[k + 1] + neighbours(zero[k])
            one[k] = (0.5 * local[k]) * zero[k] - 0.2 * beside
        for k in range(2, top - 2):
            beside = one[k - 1] + one[k + 1] + neighbours(one[k])
            two[k] = local[k] * one[k] - 0.4 * beside - zero[k]
        for k in range(3, top - 3):
            beside = two[k - 1] + two[k + 1] + neighbours(two[k])
            three[k - 3] = local[k] * two[k] - 0.4 * beside - one[k]
        for slot in range(stripes):
            start = pl.multiple_of(jnp.bitwise_xor(me, slot) * width, width)
            outs[slot][orbital] = three[:, pl.ds(start, width), :]

    first = 0
    for share, seam in zip(shares, seams):

        def step(i, carry, first=first, seam=seam):
            one_orbital(first + i, lambda k: seam[i, k])
            return carry

        lax.fori_loop(0, share, step, 0)
        first += share


def filtered_stripes(field, low, high, pots, seams, stripes):
    count, planes, rows, lanes = field.shape
    width = rows // stripes
    top = planes + 2 * DEPTH
    shares = [seam.shape[0] for seam in seams]
    shape = jax.ShapeDtypeStruct((count, planes, width, lanes), jnp.float32)
    return pl.pallas_call(
        functools.partial(filter_kernel, shares, stripes),
        out_shape=[shape] * stripes,
        scratch_shapes=[
            pltpu.VMEM((top, rows, lanes), jnp.float32),
            pltpu.VMEM((top, rows, lanes), jnp.float32),
            pltpu.VMEM((top, rows, lanes), jnp.float32),
            pltpu.VMEM((planes, rows, lanes), jnp.float32),
            pltpu.VMEM((top, rows, lanes), jnp.float32),
        ],
        compiler_params=pltpu.CompilerParams(vmem_limit_bytes=40 * 1024 * 1024),
    )(field, low, high, *pots, *seams)


def inner_pairs(step):
    half = SIDE * SIDE
    seam = half - 1 if step == 1 else 0
    return [(i, i + step) for i in range(2 * half) if i % half != seam]


def seam_pairs():
    half = SIDE * SIDE
    pairs = []
    for h in (0, 1):
        other = (1 - h) * half
        pairs += [(h * half + half - 1, other), (h * half, other + half - 1)]
    return pairs


def detour_pairs(route):
    half, last = SIDE * SIDE, SIDE - 1
    up, down = route * SIDE + last, (last - route) * SIDE
    out, back = [], []
    for h in (0, 1):
        other = (1 - h) * half
        out += [(h * half + half - 1, other + up), (h * half, other + down)]
        back += [(other + up, other), (other + down, other + half - 1)]
    return out, back


def halos(block):
    lows, highs = block[..., :DEPTH, :, :], block[..., block.shape[-3] - DEPTH :, :, :]
    low = lax.ppermute(highs, "domain", inner_pairs(1))
    high = lax.ppermute(lows, "domain", inner_pairs(-1))
    at = lax.rem(lax.axis_index("domain"), SIDE * SIDE)
    return low, high, jnp.where(at == 0, lows, highs)


def gram_kernel(pieces, cells, *rest):
    refs, (flat, gram) = rest[:-2], rest[-2:]
    me = lax.axis_index("band")
    lanes = refs[0].shape[1]
    share = refs[0].shape[0] // cells
    for index, ref in enumerate(refs):
        slot, piece = divmod(index, pieces)
        first = jnp.bitwise_xor(me, slot) * (share * pieces) + piece * share
        rows = pl.ds(pl.multiple_of(first, share), share)
        for r in range(cells):
            flat[rows, r * lanes : (r + 1) * lanes] = ref[pl.ds(r, share, stride=cells), :]
    whole = flat[...]
    gram[...] = lax.dot_general(
        whole,
        whole,
        (((1,), (1,)), ((), ())),
        precision=lax.Precision.HIGHEST,
        preferred_element_type=jnp.float32,
    )


def flat_and_gram(slots, orbitals):
    pieces = len(slots[0])
    _, planes, width, lanes = slots[0][0].shape
    cells = planes * width
    refs = [piece.reshape(-1, lanes) for slot in slots for piece in slot]
    return pl.pallas_call(
        functools.partial(gram_kernel, pieces, cells),
        out_shape=[
            jax.ShapeDtypeStruct((orbitals, cells * lanes), jnp.float32),
            jax.ShapeDtypeStruct((orbitals, orbitals), jnp.float32),
        ],
        compiler_params=pltpu.CompilerParams(vmem_limit_bytes=32 * 1024 * 1024),
    )(*refs)


def factor_kernel(panel, scale, gram, out, left, right):
    orbitals = gram.shape[0]
    row = lax.broadcasted_iota(jnp.int32, (orbitals, orbitals), 0)
    lane = lax.broadcasted_iota(jnp.int32, (orbitals, orbitals), 1)
    left[...] = gram[...]
    right[...] = jnp.where(row == lane, scale, 0.0)
    inner = lax.broadcasted_iota(jnp.int32, (panel, orbitals), 0)
    for start in range(0, orbitals, panel):
        stop = start + panel
        rows_left = left[start:stop]
        rows_right = right[start:stop]
        columns = [
            jnp.broadcast_to(rows_left[:, start + k : start + k + 1], (panel, orbitals))
            for k in range(panel)
        ]
        roots = jnp.zeros((panel, orbitals), jnp.float32)
        for j in range(panel):
            pivot = jnp.broadcast_to(columns[j][j : j + 1], (panel, orbitals))
            roots = jnp.where(inner == j, lax.rsqrt(pivot), roots)
            if j == panel - 1:
                break
            factor = jnp.where(inner > j, columns[j] / pivot, 0.0)
            for k in range(j + 1, panel):
                columns[k] = columns[k] - factor * columns[k][j : j + 1]
            rows_left = rows_left - factor * rows_left[j : j + 1]
            rows_right = rows_right - factor * rows_right[j : j + 1]
        rows_left = rows_left * roots
        rows_right = rows_right * roots
        out[start:stop] = rows_right
        if stop < orbitals:
            for ref, rows in ((left, rows_left), (right, rows_right)):
                update = lax.dot_general(
                    rows_left,
                    rows,
                    (((0,), (0,)), ((), ())),
                    precision=lax.Precision.HIGHEST,
                    preferred_element_type=jnp.float32,
                )
                ref[stop:] = ref[stop:] - update[stop:]


def scaled_inverse(gram, scale):
    orbitals = gram.shape[0]
    return pl.pallas_call(
        functools.partial(factor_kernel, PANEL, scale),
        out_shape=jax.ShapeDtypeStruct(gram.shape, jnp.float32),
        scratch_shapes=[pltpu.VMEM((orbitals, orbitals), jnp.float32)] * 2,
        compiler_params=pltpu.CompilerParams(vmem_limit_bytes=32 * 1024 * 1024),
    )(gram)


def rotate_kernel(cells, inverse, flat, out):
    orbitals = inverse.shape[0]
    lanes = out.shape[1]
    solved = jnp.dot(
        inverse[...],
        flat[...],
        precision=lax.Precision.HIGHEST,
        preferred_element_type=jnp.float32,
    )
    for r in range(cells):
        out[pl.ds(r, orbitals, stride=cells), :] = solved[:, r * lanes : (r + 1) * lanes]


def rotated(inverse, flat, lanes):
    orbitals, columns = flat.shape
    cells = columns // lanes
    return pl.pallas_call(
        functools.partial(rotate_kernel, cells),
        out_shape=jax.ShapeDtypeStruct((orbitals * cells, lanes), jnp.float32),
        compiler_params=pltpu.CompilerParams(vmem_limit_bytes=32 * 1024 * 1024),
    )(inverse, flat)


def summed(gram):
    for bit in (1, 2, 4):
        gram = gram + permuted(gram, "band", lambda i: i ^ bit)
    side = SIDE
    turned = [
        permuted(gram, "domain", lambda i: i // side * side + (i + k) % side) for k in (1, 2, 3)
    ]
    gram = (gram + turned[0]) + (turned[1] + turned[2])
    plane = side * side
    turned = [
        permuted(gram, "domain", lambda i: i // plane * plane + (i + k * side) % plane)
        for k in (1, 2, 3)
    ]
    gram = (gram + turned[0]) + (turned[1] + turned[2])
    return gram + permuted(gram, "domain", lambda i: i ^ plane)


def body(orbitals, potential):
    stripes = lax.axis_size("band")
    own, planes, ny_all, nx_all = orbitals.shape
    orb_total = own * stripes
    cell_total = planes * lax.axis_size("domain") * ny_all * nx_all

    pot_low, pot_high, pot_seam = halos(potential)
    pots = (potential, pot_low, pot_high, lax.ppermute(pot_seam, "domain", seam_pairs()))
    share = own // PARTS
    pieces = []
    for part in range(PARTS):
        field = orbitals[part * share : (part + 1) * share]
        low, high, across = halos(field)
        seams, first = [], 0
        for route, width in enumerate(SHARES):
            block = across[first : first + width]
            first += width
            if route == 0:
                seams.append(lax.ppermute(block, "domain", seam_pairs()))
            else:
                out, back = detour_pairs(route - 1)
                seams.append(lax.ppermute(lax.ppermute(block, "domain", out), "domain", back))
        slots = filtered_stripes(field, low, high, pots, seams, stripes)
        pieces.append(
            [slots[0]]
            + [permuted(slots[k], "band", lambda i: i ^ k) for k in range(1, stripes)]
        )
    slots = [[piece[k] for piece in pieces] for k in range(stripes)]
    flat, partial_gram = flat_and_gram(slots, orb_total)
    gram = summed(partial_gram)
    inverse = scaled_inverse(gram, math.sqrt(cell_total))
    return rotated(inverse, flat, nx_all).reshape(
        orb_total, planes, ny_all // stripes, nx_all
    )


def solution(mesh):
    in_specs = (P("band", "domain", None, None), P("domain", None, None))
    out_specs = P(None, "domain", "band", None)
    return jax.shard_map(body, mesh=mesh, in_specs=in_specs, out_specs=out_specs, check_vma=False)
```

```python
import functools
import math

import jax
import jax.numpy as jnp
from jax import lax
from jax.experimental import pallas as pl
from jax.experimental.pallas import tpu as pltpu
from jax.sharding import PartitionSpec as P

DEPTH = 3
PARTS = 1
PANEL = 32
SIDE = 4
SHARES = (7, 5, 4)


def permuted(block, axis, target):
    count = lax.axis_size(axis)
    return lax.ppermute(block, axis, [(i, target(i)) for i in range(count)])


def neighbours(plane):
    rows, lanes = plane.shape
    beside = pltpu.roll(plane, 1, 0) + pltpu.roll(plane, rows - 1, 0)
    return beside + pltpu.roll(plane, 1, 1) + pltpu.roll(plane, lanes - 1, 1)


def filter_kernel(shares, stripes, field, pot, low, high, *rest):
    routes = len(shares)
    seams, outs = rest[:routes], rest[routes : routes + stripes]
    zero, one, two, three, local = rest[routes + stripes :]
    me = lax.axis_index("band")
    at = lax.rem(lax.axis_index("domain"), SIDE * SIDE)
    at_low, at_high = at == 0, at == SIDE * SIDE - 1
    count, planes = field.shape[:2]
    top = planes + 2 * DEPTH
    width = outs[0].shape[2]
    own = pl.ds(DEPTH, planes)
    seam = seams[0][shares[0]]
    local[own] = 0.8 * pot[...] - 1.2
    local[:DEPTH] = 0.8 * jnp.where(at_low, seam, low[count]) - 1.2
    local[planes + DEPTH :] = 0.8 * jnp.where(at_high, seam, high[count]) - 1.2

    def one_orbital(orbital, seam_plane):
        zero[own] = field[orbital]
        for k in range(DEPTH):
            zero[k] = jnp.where(at_low, seam_plane(k), low[orbital, k])
            zero[planes + DEPTH + k] = jnp.where(at_high, seam_plane(k), high[orbital, k])
        for k in range(1, top - 1):
            beside = zero[k - 1] + zero[k + 1] + neighbours(zero[k])
            one[k] = (0.5 * local[k]) * zero[k] - 0.2 * beside
        for k in range(2, top - 2):
            beside = one[k - 1] + one[k + 1] + neighbours(one[k])
            two[k] = local[k] * one[k] - 0.4 * beside - zero[k]
        for k in range(3, top - 3):
            beside = two[k - 1] + two[k + 1] + neighbours(two[k])
            three[k - 3] = local[k] * two[k] - 0.4 * beside - one[k]
        for slot in range(stripes):
            start = pl.multiple_of(jnp.bitwise_xor(me, slot) * width, width)
            outs[slot][orbital] = three[:, pl.ds(start, width), :]

    first = 0
    for share, seam in zip(shares, seams):

        def step(i, carry, first=first, seam=seam):
            one_orbital(first + i, lambda k: seam[i, k])
            return carry

        lax.fori_loop(0, share, step, 0)
        first += share


def filtered_stripes(field, pot, low, high, seams, stripes):
    count, planes, rows, lanes = field.shape
    width = rows // stripes
    top = planes + 2 * DEPTH
    shape = jax.ShapeDtypeStruct((count, planes, width, lanes), jnp.float32)
    return pl.pallas_call(
        functools.partial(filter_kernel, SHARES, stripes),
        out_shape=[shape] * stripes,
        scratch_shapes=[
            pltpu.VMEM((top, rows, lanes), jnp.float32),
            pltpu.VMEM((top, rows, lanes), jnp.float32),
            pltpu.VMEM((top, rows, lanes), jnp.float32),
            pltpu.VMEM((planes, rows, lanes), jnp.float32),
            pltpu.VMEM((top, rows, lanes), jnp.float32),
        ],
        compiler_params=pltpu.CompilerParams(vmem_limit_bytes=40 * 1024 * 1024),
    )(field, pot, low, high, *seams)


def inner_pairs(step):
    half = SIDE * SIDE
    seam = half - 1 if step == 1 else 0
    return [(i, i + step) for i in range(2 * half) if i % half != seam]


def seam_pairs():
    half = SIDE * SIDE
    pairs = []
    for h in (0, 1):
        other = (1 - h) * half
        pairs += [(h * half + half - 1, other), (h * half, other + half - 1)]
    return pairs


def detour_pairs(route):
    half, last = SIDE * SIDE, SIDE - 1
    up, down = route * SIDE + last, (last - route) * SIDE
    out, back = [], []
    for h in (0, 1):
        other = (1 - h) * half
        out += [(h * half + half - 1, other + up), (h * half, other + down)]
        back += [(other + up, other), (other + down, other + half - 1)]
    return out, back


def halos(field, pot):
    planes = field.shape[1]
    both = jnp.concatenate([field, pot[None]])
    lows, highs = both[:, :DEPTH], both[:, planes - DEPTH :]
    at = lax.rem(lax.axis_index("domain"), SIDE * SIDE)
    across = jnp.where(at == 0, lows, highs)
    blocks, first = [], 0
    for share in SHARES:
        blocks.append(across[first : first + share])
        first += share
    blocks[0] = jnp.concatenate([blocks[0], across[first:]])
    seams = [lax.ppermute(blocks[0], "domain", seam_pairs())]
    for route, block in enumerate(blocks[1:]):
        out, back = detour_pairs(route)
        seams.append(lax.ppermute(lax.ppermute(block, "domain", out), "domain", back))
    low = lax.ppermute(highs, "domain", inner_pairs(1))
    high = lax.ppermute(lows, "domain", inner_pairs(-1))
    return low, high, seams


def gram_kernel(pieces, cells, *rest):
    refs, (flat, gram) = rest[:-2], rest[-2:]
    me = lax.axis_index("band")
    lanes = refs[0].shape[1]
    share = refs[0].shape[0] // cells
    for index, ref in enumerate(refs):
        slot, piece = divmod(index, pieces)
        first = jnp.bitwise_xor(me, slot) * (share * pieces) + piece * share
        rows = pl.ds(pl.multiple_of(first, share), share)
        for r in range(cells):
            flat[rows, r * lanes : (r + 1) * lanes] = ref[pl.ds(r, share, stride=cells), :]
    whole = flat[...]
    gram[...] = lax.dot_general(
        whole,
        whole,
        (((1,), (1,)), ((), ())),
        precision=lax.Precision.HIGHEST,
        preferred_element_type=jnp.float32,
    )


def flat_and_gram(slots, orbitals):
    pieces = len(slots[0])
    _, planes, width, lanes = slots[0][0].shape
    cells = planes * width
    refs = [piece.reshape(-1, lanes) for slot in slots for piece in slot]
    return pl.pallas_call(
        functools.partial(gram_kernel, pieces, cells),
        out_shape=[
            jax.ShapeDtypeStruct((orbitals, cells * lanes), jnp.float32),
            jax.ShapeDtypeStruct((orbitals, orbitals), jnp.float32),
        ],
        compiler_params=pltpu.CompilerParams(vmem_limit_bytes=32 * 1024 * 1024),
    )(*refs)


def factor_kernel(panel, scale, gram, out, left, right):
    orbitals = gram.shape[0]
    row = lax.broadcasted_iota(jnp.int32, (orbitals, orbitals), 0)
    lane = lax.broadcasted_iota(jnp.int32, (orbitals, orbitals), 1)
    left[...] = gram[...]
    right[...] = jnp.where(row == lane, scale, 0.0)
    inner = lax.broadcasted_iota(jnp.int32, (panel, orbitals), 0)
    for start in range(0, orbitals, panel):
        stop = start + panel
        rows_left = left[start:stop]
        rows_right = right[start:stop]
        columns = [
            jnp.broadcast_to(rows_left[:, start + k : start + k + 1], (panel, orbitals))
            for k in range(panel)
        ]
        roots = jnp.zeros((panel, orbitals), jnp.float32)
        for j in range(panel):
            pivot = jnp.broadcast_to(columns[j][j : j + 1], (panel, orbitals))
            roots = jnp.where(inner == j, lax.rsqrt(pivot), roots)
            if j == panel - 1:
                break
            factor = jnp.where(inner > j, columns[j] / pivot, 0.0)
            for k in range(j + 1, panel):
                columns[k] = columns[k] - factor * columns[k][j : j + 1]
            rows_left = rows_left - factor * rows_left[j : j + 1]
            rows_right = rows_right - factor * rows_right[j : j + 1]
        rows_left = rows_left * roots
        rows_right = rows_right * roots
        out[start:stop] = rows_right
        if stop < orbitals:
            for ref, rows in ((left, rows_left), (right, rows_right)):
                update = lax.dot_general(
                    rows_left,
                    rows,
                    (((0,), (0,)), ((), ())),
                    precision=lax.Precision.HIGHEST,
                    preferred_element_type=jnp.float32,
                )
                ref[stop:] = ref[stop:] - update[stop:]


def scaled_inverse(gram, scale):
    orbitals = gram.shape[0]
    return pl.pallas_call(
        functools.partial(factor_kernel, PANEL, scale),
        out_shape=jax.ShapeDtypeStruct(gram.shape, jnp.float32),
        scratch_shapes=[pltpu.VMEM((orbitals, orbitals), jnp.float32)] * 2,
        compiler_params=pltpu.CompilerParams(vmem_limit_bytes=32 * 1024 * 1024),
    )(gram)


def rotate_kernel(cells, inverse, flat, out):
    orbitals = inverse.shape[0]
    lanes = out.shape[1]
    solved = jnp.dot(
        inverse[...],
        flat[...],
        precision=lax.Precision.HIGHEST,
        preferred_element_type=jnp.float32,
    )
    for r in range(cells):
        out[pl.ds(r, orbitals, stride=cells), :] = solved[:, r * lanes : (r + 1) * lanes]


def rotated(inverse, flat, lanes):
    orbitals, columns = flat.shape
    cells = columns // lanes
    return pl.pallas_call(
        functools.partial(rotate_kernel, cells),
        out_shape=jax.ShapeDtypeStruct((orbitals * cells, lanes), jnp.float32),
        compiler_params=pltpu.CompilerParams(vmem_limit_bytes=32 * 1024 * 1024),
    )(inverse, flat)


def summed(gram):
    for bit in (1, 2, 4):
        gram = gram + permuted(gram, "band", lambda i: i ^ bit)
    side = SIDE
    turned = [
        permuted(gram, "domain", lambda i: i // side * side + (i + k) % side) for k in (1, 2, 3)
    ]
    gram = (gram + turned[0]) + (turned[1] + turned[2])
    plane = side * side
    turned = [
        permuted(gram, "domain", lambda i: i // plane * plane + (i + k * side) % plane)
        for k in (1, 2, 3)
    ]
    gram = (gram + turned[0]) + (turned[1] + turned[2])
    return gram + permuted(gram, "domain", lambda i: i ^ plane)


def body(orbitals, potential):
    stripes = lax.axis_size("band")
    own, planes, ny_all, nx_all = orbitals.shape
    orb_total = own * stripes
    cell_total = planes * lax.axis_size("domain") * ny_all * nx_all

    share = own // PARTS
    pieces = []
    for part in range(PARTS):
        field = orbitals[part * share : (part + 1) * share]
        low, high, seams = halos(field, potential)
        slots = filtered_stripes(field, potential, low, high, seams, stripes)
        pieces.append(
            [slots[0]]
            + [permuted(slots[k], "band", lambda i: i ^ k) for k in range(1, stripes)]
        )
    slots = [[piece[k] for piece in pieces] for k in range(stripes)]
    flat, partial_gram = flat_and_gram(slots, orb_total)
    gram = summed(partial_gram)
    inverse = scaled_inverse(gram, math.sqrt(cell_total))
    return rotated(inverse, flat, nx_all).reshape(
        orb_total, planes, ny_all // stripes, nx_all
    )


def solution(mesh):
    in_specs = (P("band", "domain", None, None), P("domain", None, None))
    out_specs = P(None, "domain", "band", None)
    return jax.shard_map(body, mesh=mesh, in_specs=in_specs, out_specs=out_specs, check_vma=False)
```

```python
import functools
import math

import jax
import jax.numpy as jnp
from jax import lax
from jax.experimental import pallas as pl
from jax.experimental.pallas import tpu as pltpu
from jax.sharding import PartitionSpec as P

DEPTH = 3
PARTS = 1
PANEL = 32
SIDE = 4
SHARES = (7, 5, 4)
DETOURS = (0, 2)


def permuted(block, axis, target):
    count = lax.axis_size(axis)
    return lax.ppermute(block, axis, [(i, target(i)) for i in range(count)])


def neighbours(plane):
    rows, lanes = plane.shape
    beside = pltpu.roll(plane, 1, 0) + pltpu.roll(plane, rows - 1, 0)
    return beside + pltpu.roll(plane, 1, 1) + pltpu.roll(plane, lanes - 1, 1)


def filter_kernel(shares, stripes, field, pot, low, high, *rest):
    routes = len(shares)
    seams, outs = rest[:routes], rest[routes : routes + stripes]
    zero, one, two, three, local = rest[routes + stripes :]
    me = lax.axis_index("band")
    at = lax.rem(lax.axis_index("domain"), SIDE * SIDE)
    at_low, at_high = at == 0, at == SIDE * SIDE - 1
    count, planes = field.shape[:2]
    top = planes + 2 * DEPTH
    width = outs[0].shape[2]
    own = pl.ds(DEPTH, planes)
    seam = seams[0][shares[0]]
    local[own] = 0.8 * pot[...] - 1.2
    local[:DEPTH] = 0.8 * jnp.where(at_low, seam, low[count]) - 1.2
    local[planes + DEPTH :] = 0.8 * jnp.where(at_high, seam, high[count]) - 1.2

    def one_orbital(orbital, seam_plane):
        zero[own] = field[orbital]
        for k in range(DEPTH):
            zero[k] = jnp.where(at_low, seam_plane(k), low[orbital, k])
            zero[planes + DEPTH + k] = jnp.where(at_high, seam_plane(k), high[orbital, k])
        for k in range(1, top - 1):
            beside = zero[k - 1] + zero[k + 1] + neighbours(zero[k])
            one[k] = (0.5 * local[k]) * zero[k] - 0.2 * beside
        for k in range(2, top - 2):
            beside = one[k - 1] + one[k + 1] + neighbours(one[k])
            two[k] = local[k] * one[k] - 0.4 * beside - zero[k]
        for k in range(3, top - 3):
            beside = two[k - 1] + two[k + 1] + neighbours(two[k])
            three[k - 3] = local[k] * two[k] - 0.4 * beside - one[k]
        for slot in range(stripes):
            start = pl.multiple_of(jnp.bitwise_xor(me, slot) * width, width)
            outs[slot][orbital] = three[:, pl.ds(start, width), :]

    first = 0
    for share, seam in zip(shares, seams):

        def step(i, carry, first=first, seam=seam):
            one_orbital(first + i, lambda k: seam[i, k])
            return carry

        lax.fori_loop(0, share, step, 0)
        first += share


def filtered_stripes(field, pot, low, high, seams, stripes):
    count, planes, rows, lanes = field.shape
    width = rows // stripes
    top = planes + 2 * DEPTH
    shape = jax.ShapeDtypeStruct((count, planes, width, lanes), jnp.float32)
    return pl.pallas_call(
        functools.partial(filter_kernel, SHARES, stripes),
        out_shape=[shape] * stripes,
        scratch_shapes=[
            pltpu.VMEM((top, rows, lanes), jnp.float32),
            pltpu.VMEM((top, rows, lanes), jnp.float32),
            pltpu.VMEM((top, rows, lanes), jnp.float32),
            pltpu.VMEM((planes, rows, lanes), jnp.float32),
            pltpu.VMEM((top, rows, lanes), jnp.float32),
        ],
        compiler_params=pltpu.CompilerParams(vmem_limit_bytes=40 * 1024 * 1024),
    )(field, pot, low, high, *seams)


def inner_pairs(step):
    half = SIDE * SIDE
    seam = half - 1 if step == 1 else 0
    return [(i, i + step) for i in range(2 * half) if i % half != seam]


def seam_pairs():
    half = SIDE * SIDE
    pairs = []
    for h in (0, 1):
        other = (1 - h) * half
        pairs += [(h * half + half - 1, other), (h * half, other + half - 1)]
    return pairs


def detour_pairs(route):
    half, last = SIDE * SIDE, SIDE - 1
    up, down = DETOURS[route] * SIDE + last, (last - DETOURS[route]) * SIDE
    out, back = [], []
    for h in (0, 1):
        own, other = h * half, (1 - h) * half
        out += [(own + half - 1, own + up), (own, own + down)]
        back += [(own + up, other), (own + down, other + half - 1)]
    return out, back


def halos(field, pot):
    planes = field.shape[1]
    both = jnp.concatenate([field, pot[None]])
    lows, highs = both[:, :DEPTH], both[:, planes - DEPTH :]
    at = lax.rem(lax.axis_index("domain"), SIDE * SIDE)
    across = jnp.where(at == 0, lows, highs)
    blocks, first = [], 0
    for share in SHARES:
        blocks.append(across[first : first + share])
        first += share
    blocks[0] = jnp.concatenate([blocks[0], across[first:]])
    seams = [lax.ppermute(blocks[0], "domain", seam_pairs())]
    for route, block in enumerate(blocks[1:]):
        out, back = detour_pairs(route)
        seams.append(lax.ppermute(lax.ppermute(block, "domain", out), "domain", back))
    low = lax.ppermute(highs, "domain", inner_pairs(1))
    high = lax.ppermute(lows, "domain", inner_pairs(-1))
    return low, high, seams


def gram_kernel(pieces, cells, *rest):
    refs, (flat, gram) = rest[:-2], rest[-2:]
    me = lax.axis_index("band")
    lanes = refs[0].shape[1]
    share = refs[0].shape[0] // cells
    for index, ref in enumerate(refs):
        slot, piece = divmod(index, pieces)
        first = jnp.bitwise_xor(me, slot) * (share * pieces) + piece * share
        rows = pl.ds(pl.multiple_of(first, share), share)
        for r in range(cells):
            flat[rows, r * lanes : (r + 1) * lanes] = ref[pl.ds(r, share, stride=cells), :]
    whole = flat[...]
    gram[...] = lax.dot_general(
        whole,
        whole,
        (((1,), (1,)), ((), ())),
        precision=lax.Precision.HIGHEST,
        preferred_element_type=jnp.float32,
    )


def flat_and_gram(slots, orbitals):
    pieces = len(slots[0])
    _, planes, width, lanes = slots[0][0].shape
    cells = planes * width
    refs = [piece.reshape(-1, lanes) for slot in slots for piece in slot]
    return pl.pallas_call(
        functools.partial(gram_kernel, pieces, cells),
        out_shape=[
            jax.ShapeDtypeStruct((orbitals, cells * lanes), jnp.float32),
            jax.ShapeDtypeStruct((orbitals, orbitals), jnp.float32),
        ],
        compiler_params=pltpu.CompilerParams(vmem_limit_bytes=32 * 1024 * 1024),
    )(*refs)


def factor_kernel(panel, scale, gram, out, left, right):
    orbitals = gram.shape[0]
    row = lax.broadcasted_iota(jnp.int32, (orbitals, orbitals), 0)
    lane = lax.broadcasted_iota(jnp.int32, (orbitals, orbitals), 1)
    left[...] = gram[...]
    right[...] = jnp.where(row == lane, scale, 0.0)
    inner = lax.broadcasted_iota(jnp.int32, (panel, orbitals), 0)
    for start in range(0, orbitals, panel):
        stop = start + panel
        rows_left = left[start:stop]
        rows_right = right[start:stop]
        columns = [
            jnp.broadcast_to(rows_left[:, start + k : start + k + 1], (panel, orbitals))
            for k in range(panel)
        ]
        roots = jnp.zeros((panel, orbitals), jnp.float32)
        for j in range(panel):
            pivot = jnp.broadcast_to(columns[j][j : j + 1], (panel, orbitals))
            roots = jnp.where(inner == j, lax.rsqrt(pivot), roots)
            if j == panel - 1:
                break
            factor = jnp.where(inner > j, columns[j] / pivot, 0.0)
            for k in range(j + 1, panel):
                columns[k] = columns[k] - factor * columns[k][j : j + 1]
            rows_left = rows_left - factor * rows_left[j : j + 1]
            rows_right = rows_right - factor * rows_right[j : j + 1]
        rows_left = rows_left * roots
        rows_right = rows_right * roots
        out[start:stop] = rows_right
        if stop < orbitals:
            for ref, rows in ((left, rows_left), (right, rows_right)):
                update = lax.dot_general(
                    rows_left,
                    rows,
                    (((0,), (0,)), ((), ())),
                    precision=lax.Precision.HIGHEST,
                    preferred_element_type=jnp.float32,
                )
                ref[stop:] = ref[stop:] - update[stop:]


def scaled_inverse(gram, scale):
    orbitals = gram.shape[0]
    return pl.pallas_call(
        functools.partial(factor_kernel, PANEL, scale),
        out_shape=jax.ShapeDtypeStruct(gram.shape, jnp.float32),
        scratch_shapes=[pltpu.VMEM((orbitals, orbitals), jnp.float32)] * 2,
        compiler_params=pltpu.CompilerParams(vmem_limit_bytes=32 * 1024 * 1024),
    )(gram)


def rotate_kernel(cells, inverse, flat, out):
    orbitals = inverse.shape[0]
    lanes = out.shape[1]
    solved = jnp.dot(
        inverse[...],
        flat[...],
        precision=lax.Precision.HIGHEST,
        preferred_element_type=jnp.float32,
    )
    for r in range(cells):
        out[pl.ds(r, orbitals, stride=cells), :] = solved[:, r * lanes : (r + 1) * lanes]


def rotated(inverse, flat, lanes):
    orbitals, columns = flat.shape
    cells = columns // lanes
    return pl.pallas_call(
        functools.partial(rotate_kernel, cells),
        out_shape=jax.ShapeDtypeStruct((orbitals * cells, lanes), jnp.float32),
        compiler_params=pltpu.CompilerParams(vmem_limit_bytes=32 * 1024 * 1024),
    )(inverse, flat)


def summed(gram):
    for bit in (1, 2, 4):
        gram = gram + permuted(gram, "band", lambda i: i ^ bit)
    side = SIDE
    turned = [
        permuted(gram, "domain", lambda i: i // side * side + (i + k) % side) for k in (1, 2, 3)
    ]
    gram = (gram + turned[0]) + (turned[1] + turned[2])
    plane = side * side
    turned = [
        permuted(gram, "domain", lambda i: i // plane * plane + (i + k * side) % plane)
        for k in (1, 2, 3)
    ]
    gram = (gram + turned[0]) + (turned[1] + turned[2])
    return gram + permuted(gram, "domain", lambda i: i ^ plane)


def body(orbitals, potential):
    stripes = lax.axis_size("band")
    own, planes, ny_all, nx_all = orbitals.shape
    orb_total = own * stripes
    cell_total = planes * lax.axis_size("domain") * ny_all * nx_all

    share = own // PARTS
    pieces = []
    for part in range(PARTS):
        field = orbitals[part * share : (part + 1) * share]
        low, high, seams = halos(field, potential)
        slots = filtered_stripes(field, potential, low, high, seams, stripes)
        pieces.append(
            [slots[0]]
            + [permuted(slots[k], "band", lambda i: i ^ k) for k in range(1, stripes)]
        )
    slots = [[piece[k] for piece in pieces] for k in range(stripes)]
    flat, partial_gram = flat_and_gram(slots, orb_total)
    gram = summed(partial_gram)
    inverse = scaled_inverse(gram, math.sqrt(cell_total))
    return rotated(inverse, flat, nx_all).reshape(
        orb_total, planes, ny_all // stripes, nx_all
    )


def solution(mesh):
    in_specs = (P("band", "domain", None, None), P("domain", None, None))
    out_specs = P(None, "domain", "band", None)
    return jax.shard_map(body, mesh=mesh, in_specs=in_specs, out_specs=out_specs, check_vma=False)
```

```python
import functools
import math

import jax
import jax.numpy as jnp
from jax import lax
from jax.experimental import pallas as pl
from jax.experimental.pallas import tpu as pltpu
from jax.sharding import PartitionSpec as P

DEPTH = 3
PARTS = 2
PANEL = 32
SIDE = 4
DETOURS = ((3, 2), (0, 1))


def permuted(block, axis, target):
    count = lax.axis_size(axis)
    return lax.ppermute(block, axis, [(i, target(i)) for i in range(count)])


def neighbours(plane):
    rows, lanes = plane.shape
    beside = pltpu.roll(plane, 1, 0) + pltpu.roll(plane, rows - 1, 0)
    return beside + pltpu.roll(plane, 1, 1) + pltpu.roll(plane, lanes - 1, 1)


def filter_kernel(shares, stripes, field, pot, pot_low, pot_high, pot_seam, low, high, *rest):
    routes = len(shares)
    seams, (out, zero, one, two, local) = rest[:routes], rest[routes:]
    at = lax.rem(lax.axis_index("domain"), SIDE * SIDE)
    at_low, at_high = at == 0, at == SIDE * SIDE - 1
    planes = field.shape[1]
    top = planes + 2 * DEPTH
    width = out.shape[3]
    own = pl.ds(DEPTH, planes)
    local[own] = 0.8 * pot[...] - 1.2
    local[:DEPTH] = 0.8 * jnp.where(at_low, pot_seam[...], pot_low[...]) - 1.2
    local[planes + DEPTH :] = 0.8 * jnp.where(at_high, pot_seam[...], pot_high[...]) - 1.2

    def one_orbital(orbital, seam_plane):
        zero[own] = field[orbital]
        for k in range(DEPTH):
            zero[k] = jnp.where(at_low, seam_plane(k), low[orbital, k])
            zero[planes + DEPTH + k] = jnp.where(at_high, seam_plane(k), high[orbital, k])
        for k in range(1, top - 1):
            beside = zero[k - 1] + zero[k + 1] + neighbours(zero[k])
            one[k] = (0.5 * local[k]) * zero[k] - 0.2 * beside
        for k in range(2, top - 2):
            beside = one[k - 1] + one[k + 1] + neighbours(one[k])
            two[k] = local[k] * one[k] - 0.4 * beside - zero[k]
        for k in range(3, top - 3):
            beside = two[k - 1] + two[k + 1] + neighbours(two[k])
            three = local[k] * two[k] - 0.4 * beside - one[k]
            for stripe in range(stripes):
                out[stripe, orbital, k - 3] = three[stripe * width : (stripe + 1) * width]

    first = 0
    for share, seam in zip(shares, seams):

        def step(i, carry, first=first, seam=seam):
            one_orbital(first + i, lambda k: seam[i, k])
            return carry

        lax.fori_loop(0, share, step, 0)
        first += share


def filtered_stripes(field, pots, low, high, seams, stripes):
    count, planes, rows, lanes = field.shape
    width = rows // stripes
    top = planes + 2 * DEPTH
    shares = [count // len(seams)] * len(seams)
    return pl.pallas_call(
        functools.partial(filter_kernel, shares, stripes),
        out_shape=jax.ShapeDtypeStruct((stripes, count, planes, width, lanes), jnp.float32),
        scratch_shapes=[
            pltpu.VMEM((top, rows, lanes), jnp.float32),
            pltpu.VMEM((top, rows, lanes), jnp.float32),
            pltpu.VMEM((top, rows, lanes), jnp.float32),
            pltpu.VMEM((top, rows, lanes), jnp.float32),
        ],
        compiler_params=pltpu.CompilerParams(vmem_limit_bytes=40 * 1024 * 1024),
    )(field, *pots, low, high, *seams)


def inner_pairs(step):
    half = SIDE * SIDE
    seam = half - 1 if step == 1 else 0
    return [(i, i + step) for i in range(2 * half) if i % half != seam]


def detour_pairs(route, bands):
    half, last = SIDE * SIDE, SIDE - 1
    out, back = [], []
    for h in (0, 1):
        own, other = h * half, (1 - h) * half
        for band in range(bands):
            column = DETOURS[route][band // 2 % 2]
            up, down = column * SIDE, (last - column) * SIDE + last
            for start, middle, end in (
                (own + half - 1, own + up, other),
                (own, own + down, other + half - 1),
            ):
                out.append((start * bands + band, middle * bands + band))
                back.append((middle * bands + band, end * bands + band))
    return out, back


def halos(block):
    bands = lax.axis_size("band")
    planes = block.shape[1]
    lows, highs = block[:, :DEPTH], block[:, planes - DEPTH :]
    at = lax.rem(lax.axis_index("domain"), SIDE * SIDE)
    across = jnp.where(at == 0, lows, highs)
    share = block.shape[0] // len(DETOURS)
    seams = []
    for route in range(len(DETOURS)):
        out, back = detour_pairs(route, bands)
        piece = across[route * share :][: share if route + 1 < len(DETOURS) else None]
        piece = lax.ppermute(piece, ("domain", "band"), out)
        seams.append(lax.ppermute(piece, ("domain", "band"), back))
    low = lax.ppermute(highs, "domain", inner_pairs(1))
    high = lax.ppermute(lows, "domain", inner_pairs(-1))
    return low, high, seams


def gram_kernel(cells, *rest):
    refs, (flat, gram) = rest[:-2], rest[-2:]
    lanes = refs[0].shape[2]
    share = refs[0].shape[1] // cells
    own = share * len(refs)
    for piece, ref in enumerate(refs):
        for band in range(ref.shape[0]):
            first = band * own + piece * share
            for r in range(cells):
                flat[first : first + share, r * lanes : (r + 1) * lanes] = ref[
                    band, pl.ds(r, share, stride=cells), :
                ]
    whole = flat[...]
    gram[...] = lax.dot_general(
        whole,
        whole,
        (((1,), (1,)), ((), ())),
        precision=lax.Precision.HIGHEST,
        preferred_element_type=jnp.float32,
    )


def flat_and_gram(pieces, orbitals):
    bands, _, planes, width, lanes = pieces[0].shape
    cells = planes * width
    refs = [piece.reshape(bands, -1, lanes) for piece in pieces]
    return pl.pallas_call(
        functools.partial(gram_kernel, cells),
        out_shape=[
            jax.ShapeDtypeStruct((orbitals, cells * lanes), jnp.float32),
            jax.ShapeDtypeStruct((orbitals, orbitals), jnp.float32),
        ],
        compiler_params=pltpu.CompilerParams(vmem_limit_bytes=32 * 1024 * 1024),
    )(*refs)


def factor_kernel(panel, scale, gram, out, left, right):
    orbitals = gram.shape[0]
    row = lax.broadcasted_iota(jnp.int32, (orbitals, orbitals), 0)
    lane = lax.broadcasted_iota(jnp.int32, (orbitals, orbitals), 1)
    left[...] = gram[...]
    right[...] = jnp.where(row == lane, scale, 0.0)
    inner = lax.broadcasted_iota(jnp.int32, (panel, orbitals), 0)
    for start in range(0, orbitals, panel):
        stop = start + panel
        rows_left = left[start:stop]
        rows_right = right[start:stop]
        columns = [
            jnp.broadcast_to(rows_left[:, start + k : start + k + 1], (panel, orbitals))
            for k in range(panel)
        ]
        roots = jnp.zeros((panel, orbitals), jnp.float32)
        for j in range(panel):
            pivot = jnp.broadcast_to(columns[j][j : j + 1], (panel, orbitals))
            roots = jnp.where(inner == j, lax.rsqrt(pivot), roots)
            if j == panel - 1:
                break
            factor = jnp.where(inner > j, columns[j] / pivot, 0.0)
            for k in range(j + 1, panel):
                columns[k] = columns[k] - factor * columns[k][j : j + 1]
            rows_left = rows_left - factor * rows_left[j : j + 1]
            rows_right = rows_right - factor * rows_right[j : j + 1]
        rows_left = rows_left * roots
        rows_right = rows_right * roots
        out[start:stop] = rows_right
        if stop < orbitals:
            for ref, rows in ((left, rows_left), (right, rows_right)):
                update = lax.dot_general(
                    rows_left,
                    rows,
                    (((0,), (0,)), ((), ())),
                    precision=lax.Precision.HIGHEST,
                    preferred_element_type=jnp.float32,
                )
                ref[stop:] = ref[stop:] - update[stop:]


def scaled_inverse(gram, scale):
    orbitals = gram.shape[0]
    return pl.pallas_call(
        functools.partial(factor_kernel, PANEL, scale),
        out_shape=jax.ShapeDtypeStruct(gram.shape, jnp.float32),
        scratch_shapes=[pltpu.VMEM((orbitals, orbitals), jnp.float32)] * 2,
        compiler_params=pltpu.CompilerParams(vmem_limit_bytes=32 * 1024 * 1024),
    )(gram)


def rotate_kernel(cells, inverse, flat, out):
    orbitals = inverse.shape[0]
    lanes = out.shape[1]
    solved = jnp.dot(
        inverse[...],
        flat[...],
        precision=lax.Precision.HIGHEST,
        preferred_element_type=jnp.float32,
    )
    for r in range(cells):
        out[pl.ds(r, orbitals, stride=cells), :] = solved[:, r * lanes : (r + 1) * lanes]


def rotated(inverse, flat, lanes):
    orbitals, columns = flat.shape
    cells = columns // lanes
    return pl.pallas_call(
        functools.partial(rotate_kernel, cells),
        out_shape=jax.ShapeDtypeStruct((orbitals * cells, lanes), jnp.float32),
        compiler_params=pltpu.CompilerParams(vmem_limit_bytes=32 * 1024 * 1024),
    )(inverse, flat)


def summed(gram):
    for bit in (1, 2, 4):
        gram = gram + permuted(gram, "band", lambda i: i ^ bit)
    side = SIDE
    turned = [
        permuted(gram, "domain", lambda i: i // side * side + (i + k) % side) for k in (1, 2, 3)
    ]
    gram = (gram + turned[0]) + (turned[1] + turned[2])
    plane = side * side
    turned = [
        permuted(gram, "domain", lambda i: i // plane * plane + (i + k * side) % plane)
        for k in (1, 2, 3)
    ]
    gram = (gram + turned[0]) + (turned[1] + turned[2])
    return gram + permuted(gram, "domain", lambda i: i ^ plane)


def body(orbitals, potential):
    stripes = lax.axis_size("band")
    own, planes, ny_all, nx_all = orbitals.shape
    orb_total = own * stripes
    cell_total = planes * lax.axis_size("domain") * ny_all * nx_all

    share = own // PARTS
    pieces = []
    for part in range(PARTS):
        field = orbitals[part * share : (part + 1) * share]
        if part == 0:
            low, high, seams = halos(jnp.concatenate([field, potential[None]]))
            pots = (potential, low[share], high[share], seams[-1][-1])
        else:
            low, high, seams = halos(field)
        striped = filtered_stripes(field, pots, low, high, seams, stripes)
        pieces.append(lax.all_to_all(striped, "band", 0, 0, tiled=True))
    flat, partial_gram = flat_and_gram(pieces, orb_total)
    gram = summed(partial_gram)
    inverse = scaled_inverse(gram, math.sqrt(cell_total))
    return rotated(inverse, flat, nx_all).reshape(
        orb_total, planes, ny_all // stripes, nx_all
    )


def solution(mesh):
    in_specs = (P("band", "domain", None, None), P("domain", None, None))
    out_specs = P(None, "domain", "band", None)
    return jax.shard_map(body, mesh=mesh, in_specs=in_specs, out_specs=out_specs, check_vma=False)
```

```python
import functools
import math

import jax
import jax.numpy as jnp
from jax import lax
from jax.experimental import pallas as pl
from jax.experimental.pallas import tpu as pltpu
from jax.sharding import PartitionSpec as P

DEPTH = 3
PARTS = 1
PANEL = 32
SIDE = 4
SHARES = (8, 4, 4)
DETOURS = (0, 2)


def permuted(block, axis, target):
    count = lax.axis_size(axis)
    return lax.ppermute(block, axis, [(i, target(i)) for i in range(count)])


def neighbours(plane):
    rows, lanes = plane.shape
    beside = pltpu.roll(plane, 1, 0) + pltpu.roll(plane, rows - 1, 0)
    return beside + pltpu.roll(plane, 1, 1) + pltpu.roll(plane, lanes - 1, 1)


def filter_kernel(shares, stripes, field, pot, low, high, *rest):
    routes = len(shares)
    seams, outs = rest[:routes], rest[routes : routes + stripes]
    zero, one, two, three, local = rest[routes + stripes :]
    me = lax.axis_index("band")
    at = lax.rem(lax.axis_index("domain"), SIDE * SIDE)
    at_low, at_high = at == 0, at == SIDE * SIDE - 1
    count, planes = field.shape[:2]
    top = planes + 2 * DEPTH
    width = outs[0].shape[2]
    own = pl.ds(DEPTH, planes)
    seam = seams[0][shares[0]]
    local[own] = 0.8 * pot[...] - 1.2
    local[:DEPTH] = 0.8 * jnp.where(at_low, seam, low[count]) - 1.2
    local[planes + DEPTH :] = 0.8 * jnp.where(at_high, seam, high[count]) - 1.2

    def one_orbital(orbital, seam_plane):
        zero[own] = field[orbital]
        for k in range(DEPTH):
            zero[k] = jnp.where(at_low, seam_plane(k), low[orbital, k])
            zero[planes + DEPTH + k] = jnp.where(at_high, seam_plane(k), high[orbital, k])
        for k in range(1, top - 1):
            beside = zero[k - 1] + zero[k + 1] + neighbours(zero[k])
            one[k] = (0.5 * local[k]) * zero[k] - 0.2 * beside
        for k in range(2, top - 2):
            beside = one[k - 1] + one[k + 1] + neighbours(one[k])
            two[k] = local[k] * one[k] - 0.4 * beside - zero[k]
        for k in range(3, top - 3):
            beside = two[k - 1] + two[k + 1] + neighbours(two[k])
            three[k - 3] = local[k] * two[k] - 0.4 * beside - one[k]
        for slot in range(stripes):
            start = pl.multiple_of(jnp.bitwise_xor(me, slot) * width, width)
            outs[slot][orbital] = three[:, pl.ds(start, width), :]

    first = 0
    for share, seam in zip(shares, seams):

        def step(i, carry, first=first, seam=seam):
            one_orbital(first + i, lambda k: seam[i, k])
            return carry

        lax.fori_loop(0, share, step, 0)
        first += share


def filtered_stripes(field, pot, low, high, seams, stripes):
    count, planes, rows, lanes = field.shape
    width = rows // stripes
    top = planes + 2 * DEPTH
    shape = jax.ShapeDtypeStruct((count, planes, width, lanes), jnp.float32)
    return pl.pallas_call(
        functools.partial(filter_kernel, SHARES, stripes),
        out_shape=[shape] * stripes,
        scratch_shapes=[
            pltpu.VMEM((top, rows, lanes), jnp.float32),
            pltpu.VMEM((top, rows, lanes), jnp.float32),
            pltpu.VMEM((top, rows, lanes), jnp.float32),
            pltpu.VMEM((planes, rows, lanes), jnp.float32),
            pltpu.VMEM((top, rows, lanes), jnp.float32),
        ],
        compiler_params=pltpu.CompilerParams(vmem_limit_bytes=40 * 1024 * 1024),
    )(field, pot, low, high, *seams)


def inner_pairs(step):
    half = SIDE * SIDE
    seam = half - 1 if step == 1 else 0
    return [(i, i + step) for i in range(2 * half) if i % half != seam]


def seam_pairs():
    half = SIDE * SIDE
    pairs = []
    for h in (0, 1):
        other = (1 - h) * half
        pairs += [(h * half + half - 1, other), (h * half, other + half - 1)]
    return pairs


def detour_pairs(route):
    half, last = SIDE * SIDE, SIDE - 1
    up, down = DETOURS[route] * SIDE + last, (last - DETOURS[route]) * SIDE
    out, back = [], []
    for h in (0, 1):
        own, other = h * half, (1 - h) * half
        out += [(own + half - 1, own + up), (own, own + down)]
        back += [(own + up, other), (own + down, other + half - 1)]
    return out, back


def halos(field, pot):
    planes = field.shape[1]
    at = lax.rem(lax.axis_index("domain"), SIDE * SIDE)

    def across(first, stop):
        block = field[first:stop]
        return jnp.where(at == 0, block[:, :DEPTH], block[:, planes - DEPTH :])

    blocks, first = [], 0
    for share in SHARES:
        blocks.append(across(first, first + share))
        first += share
    last = jnp.where(at == 0, pot[:DEPTH], pot[planes - DEPTH :])
    blocks[0] = jnp.concatenate([blocks[0], last[None]])
    seams = [lax.ppermute(blocks[0], "domain", seam_pairs())]
    for route, block in enumerate(blocks[1:]):
        out, back = detour_pairs(route)
        seams.append(lax.ppermute(lax.ppermute(block, "domain", out), "domain", back))
    field, pot, *_ = lax.optimization_barrier((field, pot, *blocks))
    both = jnp.concatenate([field, pot[None]])
    low = lax.ppermute(both[:, planes - DEPTH :], "domain", inner_pairs(1))
    high = lax.ppermute(both[:, :DEPTH], "domain", inner_pairs(-1))
    return low, high, seams


def gram_kernel(pieces, cells, *rest):
    refs, (flat, gram) = rest[:-2], rest[-2:]
    me = lax.axis_index("band")
    lanes = refs[0].shape[1]
    share = refs[0].shape[0] // cells
    for index, ref in enumerate(refs):
        slot, piece = divmod(index, pieces)
        first = jnp.bitwise_xor(me, slot) * (share * pieces) + piece * share
        rows = pl.ds(pl.multiple_of(first, share), share)
        for r in range(cells):
            flat[rows, r * lanes : (r + 1) * lanes] = ref[pl.ds(r, share, stride=cells), :]
    whole = flat[...]
    gram[...] = lax.dot_general(
        whole,
        whole,
        (((1,), (1,)), ((), ())),
        precision=lax.Precision.HIGHEST,
        preferred_element_type=jnp.float32,
    )


def flat_and_gram(slots, orbitals):
    pieces = len(slots[0])
    _, planes, width, lanes = slots[0][0].shape
    cells = planes * width
    refs = [piece.reshape(-1, lanes) for slot in slots for piece in slot]
    return pl.pallas_call(
        functools.partial(gram_kernel, pieces, cells),
        out_shape=[
            jax.ShapeDtypeStruct((orbitals, cells * lanes), jnp.float32),
            jax.ShapeDtypeStruct((orbitals, orbitals), jnp.float32),
        ],
        compiler_params=pltpu.CompilerParams(vmem_limit_bytes=32 * 1024 * 1024),
    )(*refs)


def factor_kernel(panel, scale, gram, out, left, right):
    orbitals = gram.shape[0]
    row = lax.broadcasted_iota(jnp.int32, (orbitals, orbitals), 0)
    lane = lax.broadcasted_iota(jnp.int32, (orbitals, orbitals), 1)
    left[...] = gram[...]
    right[...] = jnp.where(row == lane, scale, 0.0)
    inner = lax.broadcasted_iota(jnp.int32, (panel, orbitals), 0)
    for start in range(0, orbitals, panel):
        stop = start + panel
        rows_left = left[start:stop]
        rows_right = right[start:stop]
        columns = [
            jnp.broadcast_to(rows_left[:, start + k : start + k + 1], (panel, orbitals))
            for k in range(panel)
        ]
        roots = jnp.zeros((panel, orbitals), jnp.float32)
        for j in range(panel):
            pivot = jnp.broadcast_to(columns[j][j : j + 1], (panel, orbitals))
            roots = jnp.where(inner == j, lax.rsqrt(pivot), roots)
            if j == panel - 1:
                break
            factor = jnp.where(inner > j, columns[j] / pivot, 0.0)
            for k in range(j + 1, panel):
                columns[k] = columns[k] - factor * columns[k][j : j + 1]
            rows_left = rows_left - factor * rows_left[j : j + 1]
            rows_right = rows_right - factor * rows_right[j : j + 1]
        rows_left = rows_left * roots
        rows_right = rows_right * roots
        out[start:stop] = rows_right
        if stop < orbitals:
            for ref, rows in ((left, rows_left), (right, rows_right)):
                update = lax.dot_general(
                    rows_left,
                    rows,
                    (((0,), (0,)), ((), ())),
                    precision=lax.Precision.HIGHEST,
                    preferred_element_type=jnp.float32,
                )
                ref[stop:] = ref[stop:] - update[stop:]


def scaled_inverse(gram, scale):
    orbitals = gram.shape[0]
    return pl.pallas_call(
        functools.partial(factor_kernel, PANEL, scale),
        out_shape=jax.ShapeDtypeStruct(gram.shape, jnp.float32),
        scratch_shapes=[pltpu.VMEM((orbitals, orbitals), jnp.float32)] * 2,
        compiler_params=pltpu.CompilerParams(vmem_limit_bytes=32 * 1024 * 1024),
    )(gram)


def rotate_kernel(cells, inverse, flat, out):
    orbitals = inverse.shape[0]
    lanes = out.shape[1]
    solved = jnp.dot(
        inverse[...],
        flat[...],
        precision=lax.Precision.HIGHEST,
        preferred_element_type=jnp.float32,
    )
    for r in range(cells):
        out[pl.ds(r, orbitals, stride=cells), :] = solved[:, r * lanes : (r + 1) * lanes]


def rotated(inverse, flat, lanes):
    orbitals, columns = flat.shape
    cells = columns // lanes
    return pl.pallas_call(
        functools.partial(rotate_kernel, cells),
        out_shape=jax.ShapeDtypeStruct((orbitals * cells, lanes), jnp.float32),
        compiler_params=pltpu.CompilerParams(vmem_limit_bytes=32 * 1024 * 1024),
    )(inverse, flat)


def summed(gram):
    for bit in (1, 2, 4):
        gram = gram + permuted(gram, "band", lambda i: i ^ bit)
    side = SIDE
    turned = [
        permuted(gram, "domain", lambda i: i // side * side + (i + k) % side) for k in (1, 2, 3)
    ]
    gram = (gram + turned[0]) + (turned[1] + turned[2])
    plane = side * side
    turned = [
        permuted(gram, "domain", lambda i: i // plane * plane + (i + k * side) % plane)
        for k in (1, 2, 3)
    ]
    gram = (gram + turned[0]) + (turned[1] + turned[2])
    return gram + permuted(gram, "domain", lambda i: i ^ plane)


def body(orbitals, potential):
    stripes = lax.axis_size("band")
    own, planes, ny_all, nx_all = orbitals.shape
    orb_total = own * stripes
    cell_total = planes * lax.axis_size("domain") * ny_all * nx_all

    share = own // PARTS
    pieces = []
    for part in range(PARTS):
        field = orbitals[part * share : (part + 1) * share]
        low, high, seams = halos(field, potential)
        slots = filtered_stripes(field, potential, low, high, seams, stripes)
        pieces.append(
            [slots[0]]
            + [permuted(slots[k], "band", lambda i: i ^ k) for k in range(1, stripes)]
        )
    slots = [[piece[k] for piece in pieces] for k in range(stripes)]
    flat, partial_gram = flat_and_gram(slots, orb_total)
    gram = summed(partial_gram)
    inverse = scaled_inverse(gram, math.sqrt(cell_total))
    return rotated(inverse, flat, nx_all).reshape(
        orb_total, planes, ny_all // stripes, nx_all
    )


def solution(mesh):
    in_specs = (P("band", "domain", None, None), P("domain", None, None))
    out_specs = P(None, "domain", "band", None)
    return jax.shard_map(body, mesh=mesh, in_specs=in_specs, out_specs=out_specs, check_vma=False)
```

```python
import functools
import math

import jax
import jax.numpy as jnp
from jax import lax
from jax.experimental import pallas as pl
from jax.experimental.pallas import tpu as pltpu
from jax.sharding import PartitionSpec as P

DEPTH = 3
TIED = True
EARLY = (7, 6, 5)
PANEL = 32
SIDE = 4
SHARES = (8, 4, 4)
DETOURS = (0, 2)


def permuted(block, axis, target):
    count = lax.axis_size(axis)
    return lax.ppermute(block, axis, [(i, target(i)) for i in range(count)])


def neighbours(plane):
    rows, lanes = plane.shape
    beside = pltpu.roll(plane, 1, 0) + pltpu.roll(plane, rows - 1, 0)
    return beside + pltpu.roll(plane, 1, 1) + pltpu.roll(plane, lanes - 1, 1)


def filter_kernel(begin, shares, stripes, field, pot, pot_low, pot_high, pot_seam, low, high, *rest):
    routes = len(shares)
    seams, outs = rest[:routes], rest[routes : routes + stripes]
    zero, one, two, three, local = rest[routes + stripes :]
    me = lax.axis_index("band")
    at = lax.rem(lax.axis_index("domain"), SIDE * SIDE)
    at_low, at_high = at == 0, at == SIDE * SIDE - 1
    planes = field.shape[1]
    top = planes + 2 * DEPTH
    width = outs[0].shape[2]
    own = pl.ds(DEPTH, planes)
    local[own] = 0.8 * pot[...] - 1.2
    local[:DEPTH] = 0.8 * jnp.where(at_low, pot_seam[...], pot_low[...]) - 1.2
    local[planes + DEPTH :] = 0.8 * jnp.where(at_high, pot_seam[...], pot_high[...]) - 1.2

    def one_orbital(orbital, seam_plane):
        zero[own] = field[orbital]
        for k in range(DEPTH):
            zero[k] = jnp.where(at_low, seam_plane(k), low[begin + orbital, k])
            zero[planes + DEPTH + k] = jnp.where(at_high, seam_plane(k), high[begin + orbital, k])
        for k in range(1, top - 1):
            beside = zero[k - 1] + zero[k + 1] + neighbours(zero[k])
            one[k] = (0.5 * local[k]) * zero[k] - 0.2 * beside
        for k in range(2, top - 2):
            beside = one[k - 1] + one[k + 1] + neighbours(one[k])
            two[k] = local[k] * one[k] - 0.4 * beside - zero[k]
        for k in range(3, top - 3):
            beside = two[k - 1] + two[k + 1] + neighbours(two[k])
            three[k - 3] = local[k] * two[k] - 0.4 * beside - one[k]
        for slot in range(stripes):
            start = pl.multiple_of(jnp.bitwise_xor(me, slot) * width, width)
            outs[slot][orbital] = three[:, pl.ds(start, width), :]

    first = 0
    for share, seam in zip(shares, seams):

        def step(i, carry, first=first, seam=seam):
            one_orbital(first + i, lambda k: seam[i, k])
            return carry

        lax.fori_loop(0, share, step, 0)
        first += share


def filtered_stripes(field, pots, low, high, begin, seams, stripes):
    count, planes, rows, lanes = field.shape
    width = rows // stripes
    top = planes + 2 * DEPTH
    shares = [min(seam.shape[0], count) for seam in seams]
    shape = jax.ShapeDtypeStruct((count, planes, width, lanes), jnp.float32)
    return pl.pallas_call(
        functools.partial(filter_kernel, begin, shares, stripes),
        out_shape=[shape] * stripes,
        scratch_shapes=[
            pltpu.VMEM((top, rows, lanes), jnp.float32),
            pltpu.VMEM((top, rows, lanes), jnp.float32),
            pltpu.VMEM((top, rows, lanes), jnp.float32),
            pltpu.VMEM((planes, rows, lanes), jnp.float32),
            pltpu.VMEM((top, rows, lanes), jnp.float32),
        ],
        compiler_params=pltpu.CompilerParams(vmem_limit_bytes=40 * 1024 * 1024),
    )(field, *pots, low, high, *seams)


def inner_pairs(step):
    half = SIDE * SIDE
    seam = half - 1 if step == 1 else 0
    return [(i, i + step) for i in range(2 * half) if i % half != seam]


def seam_pairs():
    half = SIDE * SIDE
    pairs = []
    for h in (0, 1):
        other = (1 - h) * half
        pairs += [(h * half + half - 1, other), (h * half, other + half - 1)]
    return pairs


def detour_pairs(route):
    half, last = SIDE * SIDE, SIDE - 1
    up, down = DETOURS[route] * SIDE + last, (last - DETOURS[route]) * SIDE
    out, back = [], []
    for h in (0, 1):
        own, other = h * half, (1 - h) * half
        out += [(own + half - 1, own + up), (own, own + down)]
        back += [(own + up, other), (own + down, other + half - 1)]
    return out, back


def halos(field, pot):
    planes = field.shape[1]
    at = lax.rem(lax.axis_index("domain"), SIDE * SIDE)

    def across(first, stop):
        block = field[first:stop]
        return jnp.where(at == 0, block[:, :DEPTH], block[:, planes - DEPTH :])

    blocks, first = [], 0
    for share in SHARES:
        blocks.append(across(first, first + share))
        first += share
    last = jnp.where(at == 0, pot[:DEPTH], pot[planes - DEPTH :])
    blocks[0] = jnp.concatenate([blocks[0], last[None]])
    seams = [lax.ppermute(blocks[0], "domain", seam_pairs())]
    for route, block in enumerate(blocks[1:]):
        out, back = detour_pairs(route)
        seams.append(lax.ppermute(lax.ppermute(block, "domain", out), "domain", back))
    field, pot, *_ = lax.optimization_barrier((field, pot, *blocks))
    both = jnp.concatenate([field, pot[None]])
    low = lax.ppermute(both[:, planes - DEPTH :], "domain", inner_pairs(1))
    high = lax.ppermute(both[:, :DEPTH], "domain", inner_pairs(-1))
    return low, high, seams


def gram_kernel(pieces, cells, *rest):
    refs, (flat, own, other, gram) = rest[:-4], rest[-4:]
    me = lax.axis_index("band")
    lanes = refs[0].shape[1]
    share = refs[0].shape[0] // cells
    for index, ref in enumerate(refs):
        slot, piece = divmod(index, pieces)
        first = jnp.bitwise_xor(me, slot) * (share * pieces) + piece * share
        rows = pl.ds(pl.multiple_of(first, share), share)
        for r in range(cells):
            flat[rows, r * lanes : (r + 1) * lanes] = ref[pl.ds(r, share, stride=cells), :]
    whole = flat[...]
    gram[...] = lax.dot_general(
        whole,
        whole,
        (((1,), (1,)), ((), ())),
        precision=lax.Precision.HIGHEST,
        preferred_element_type=jnp.float32,
    )
    half = gram.shape[0] // 2
    core = lax.rem(lax.axis_index("band"), 2)
    own[...] = gram[pl.ds(pl.multiple_of(core * half, half), half)]
    other[...] = gram[pl.ds(pl.multiple_of((1 - core) * half, half), half)]


def flat_and_gram(slots, orbitals):
    pieces = len(slots[0])
    _, planes, width, lanes = slots[0][0].shape
    cells = planes * width
    refs = [piece.reshape(-1, lanes) for slot in slots for piece in slot]
    return pl.pallas_call(
        functools.partial(gram_kernel, pieces, cells),
        out_shape=[
            jax.ShapeDtypeStruct((orbitals, cells * lanes), jnp.float32),
            jax.ShapeDtypeStruct((orbitals // 2, orbitals), jnp.float32),
            jax.ShapeDtypeStruct((orbitals // 2, orbitals), jnp.float32),
        ],
        scratch_shapes=[pltpu.VMEM((orbitals, orbitals), jnp.float32)],
        compiler_params=pltpu.CompilerParams(vmem_limit_bytes=32 * 1024 * 1024),
    )(*refs)


def factor_kernel(panel, scale, own, other, out, left, right):
    half, orbitals = own.shape
    core = lax.rem(lax.axis_index("band"), 2)
    row = lax.broadcasted_iota(jnp.int32, (orbitals, orbitals), 0)
    lane = lax.broadcasted_iota(jnp.int32, (orbitals, orbitals), 1)
    left[pl.ds(pl.multiple_of(core * half, half), half)] = own[...]
    left[pl.ds(pl.multiple_of((1 - core) * half, half), half)] = other[...]
    right[...] = jnp.where(row == lane, scale, 0.0)
    inner = lax.broadcasted_iota(jnp.int32, (panel, orbitals), 0)
    for start in range(0, orbitals, panel):
        stop = start + panel
        rows_left = left[start:stop]
        rows_right = right[start:stop]
        columns = [
            jnp.broadcast_to(rows_left[:, start + k : start + k + 1], (panel, orbitals))
            for k in range(panel)
        ]
        roots = jnp.zeros((panel, orbitals), jnp.float32)
        for j in range(panel):
            pivot = jnp.broadcast_to(columns[j][j : j + 1], (panel, orbitals))
            roots = jnp.where(inner == j, lax.rsqrt(pivot), roots)
            if j == panel - 1:
                break
            factor = jnp.where(inner > j, columns[j] / pivot, 0.0)
            for k in range(j + 1, panel):
                columns[k] = columns[k] - factor * columns[k][j : j + 1]
            rows_left = rows_left - factor * rows_left[j : j + 1]
            rows_right = rows_right - factor * rows_right[j : j + 1]
        rows_left = rows_left * roots
        rows_right = rows_right * roots
        out[start:stop] = rows_right
        if stop < orbitals:
            for ref, rows in ((left, rows_left), (right, rows_right)):
                update = lax.dot_general(
                    rows_left,
                    rows,
                    (((0,), (0,)), ((), ())),
                    precision=lax.Precision.HIGHEST,
                    preferred_element_type=jnp.float32,
                )
                ref[stop:] = ref[stop:] - update[stop:]


def scaled_inverse(own, other, scale):
    orbitals = own.shape[1]
    return pl.pallas_call(
        functools.partial(factor_kernel, PANEL, scale),
        out_shape=jax.ShapeDtypeStruct((orbitals, orbitals), jnp.float32),
        scratch_shapes=[pltpu.VMEM((orbitals, orbitals), jnp.float32)] * 2,
        compiler_params=pltpu.CompilerParams(vmem_limit_bytes=32 * 1024 * 1024),
    )(own, other)


def rotate_kernel(cells, inverse, flat, out):
    orbitals = inverse.shape[0]
    lanes = out.shape[1]
    solved = jnp.dot(
        inverse[...],
        flat[...],
        precision=lax.Precision.HIGHEST,
        preferred_element_type=jnp.float32,
    )
    for r in range(cells):
        out[pl.ds(r, orbitals, stride=cells), :] = solved[:, r * lanes : (r + 1) * lanes]


def rotated(inverse, flat, lanes):
    orbitals, columns = flat.shape
    cells = columns // lanes
    return pl.pallas_call(
        functools.partial(rotate_kernel, cells),
        out_shape=jax.ShapeDtypeStruct((orbitals * cells, lanes), jnp.float32),
        compiler_params=pltpu.CompilerParams(vmem_limit_bytes=32 * 1024 * 1024),
    )(inverse, flat)


def summed(own, other):
    bands, half = lax.axis_size("band"), SIDE * SIDE
    depth = lax.axis_size("domain") // half * bands // 2

    def along_z(block, step):
        pairs = []
        for domain in range(lax.axis_size("domain")):
            for band in range(bands):
                z = (domain // half * (bands // 2) + band // 2 + step) % depth
                there = z // (bands // 2) * half + domain % half
                pairs.append((domain * bands + band, there * bands + z % (bands // 2) * 2 + band % 2))
        return lax.ppermute(block, ("domain", "band"), pairs)

    def turned(block, target):
        parts = [permuted(block, "domain", lambda i: target(i, k)) for k in (1, 2, 3)]
        return (block + parts[0]) + (parts[1] + parts[2])

    own = own + permuted(other, "band", lambda i: i ^ 1)
    own = own + permuted(own, "band", lambda i: i ^ 2)
    parts = [along_z(own, step) for step in (2, -2, 4)]
    own = (own + parts[2]) + (parts[0] + parts[1])
    own = turned(own, lambda i, k: i // SIDE * SIDE + (i + k) % SIDE)
    own = turned(own, lambda i, k: i // half * half + (i + k * SIDE) % half)
    return own, permuted(own, "band", lambda i: i ^ 1)


def body(orbitals, potential):
    stripes = lax.axis_size("band")
    own, planes, ny_all, nx_all = orbitals.shape
    orb_total = own * stripes
    cell_total = planes * lax.axis_size("domain") * ny_all * nx_all

    cut = SHARES[0]
    low, high, (seam, *others) = halos(orbitals, potential)
    pots = (potential, low[own], high[own], seam[cut])

    def sent(slots, chosen):
        return [permuted(slots[k], "band", lambda i: i ^ k) for k in chosen]

    slots = filtered_stripes(orbitals[:cut], pots, low, high, 0, [seam], stripes)
    early = sent(slots, EARLY)
    count = len(others)
    if TIED:
        tied = lax.optimization_barrier((*others, *early))
        others, early = tied[:count], list(tied[count:])
    rest = [k for k in range(1, stripes) if k not in EARLY]
    first = dict(zip([0, *EARLY, *rest], [slots[0], *early, *sent(slots, rest)]))
    slots = filtered_stripes(orbitals[cut:], pots, low, high, cut, others, stripes)
    second = [slots[0], *sent(slots, range(1, stripes))]
    slots = [[first[k], second[k]] for k in range(stripes)]
    flat, own_half, other_half = flat_and_gram(slots, orb_total)
    inverse = scaled_inverse(*summed(own_half, other_half), math.sqrt(cell_total))
    return rotated(inverse, flat, nx_all).reshape(
        orb_total, planes, ny_all // stripes, nx_all
    )


def solution(mesh):
    in_specs = (P("band", "domain", None, None), P("domain", None, None))
    out_specs = P(None, "domain", "band", None)
    return jax.shard_map(body, mesh=mesh, in_specs=in_specs, out_specs=out_specs, check_vma=False)
```

```python
import functools
import math

import jax
import jax.numpy as jnp
from jax import lax
from jax.experimental import pallas as pl
from jax.experimental.pallas import tpu as pltpu
from jax.sharding import PartitionSpec as P

DEPTH = 3
TIED = True
EARLY = (6,)
PANEL = 32
SIDE = 4
SHARES = (8, 4, 4)
DETOURS = (0, 2)


def permuted(block, axis, target):
    count = lax.axis_size(axis)
    return lax.ppermute(block, axis, [(i, target(i)) for i in range(count)])


def neighbours(plane):
    rows, lanes = plane.shape
    beside = pltpu.roll(plane, 1, 0) + pltpu.roll(plane, rows - 1, 0)
    return beside + pltpu.roll(plane, 1, 1) + pltpu.roll(plane, lanes - 1, 1)


def filter_kernel(begin, shares, stripes, field, pot, pot_low, pot_high, pot_seam, low, high, *rest):
    routes = len(shares)
    seams, outs = rest[:routes], rest[routes : routes + stripes]
    zero, one, two, three, local = rest[routes + stripes :]
    me = lax.axis_index("band")
    at = lax.rem(lax.axis_index("domain"), SIDE * SIDE)
    at_low, at_high = at == 0, at == SIDE * SIDE - 1
    planes = field.shape[1]
    top = planes + 2 * DEPTH
    width = outs[0].shape[2]
    own = pl.ds(DEPTH, planes)
    local[own] = 0.8 * pot[...] - 1.2
    local[:DEPTH] = 0.8 * jnp.where(at_low, pot_seam[...], pot_low[...]) - 1.2
    local[planes + DEPTH :] = 0.8 * jnp.where(at_high, pot_seam[...], pot_high[...]) - 1.2

    def one_orbital(orbital, seam_plane):
        zero[own] = field[orbital]
        for k in range(DEPTH):
            zero[k] = jnp.where(at_low, seam_plane(k), low[begin + orbital, k])
            zero[planes + DEPTH + k] = jnp.where(at_high, seam_plane(k), high[begin + orbital, k])
        for k in range(1, top - 1):
            beside = zero[k - 1] + zero[k + 1] + neighbours(zero[k])
            one[k] = (0.5 * local[k]) * zero[k] - 0.2 * beside
        for k in range(2, top - 2):
            beside = one[k - 1] + one[k + 1] + neighbours(one[k])
            two[k] = local[k] * one[k] - 0.4 * beside - zero[k]
        for k in range(3, top - 3):
            beside = two[k - 1] + two[k + 1] + neighbours(two[k])
            three[k - 3] = local[k] * two[k] - 0.4 * beside - one[k]
        for slot in range(stripes):
            start = pl.multiple_of(jnp.bitwise_xor(me, slot) * width, width)
            outs[slot][orbital] = three[:, pl.ds(start, width), :]

    first = 0
    for share, seam in zip(shares, seams):

        def step(i, carry, first=first, seam=seam):
            one_orbital(first + i, lambda k: seam[i, k])
            return carry

        lax.fori_loop(0, share, step, 0)
        first += share


def filtered_stripes(field, pots, low, high, begin, seams, stripes):
    count, planes, rows, lanes = field.shape
    width = rows // stripes
    top = planes + 2 * DEPTH
    shares = [min(seam.shape[0], count) for seam in seams]
    shape = jax.ShapeDtypeStruct((count, planes, width, lanes), jnp.float32)
    return pl.pallas_call(
        functools.partial(filter_kernel, begin, shares, stripes),
        out_shape=[shape] * stripes,
        scratch_shapes=[
            pltpu.VMEM((top, rows, lanes), jnp.float32),
            pltpu.VMEM((top, rows, lanes), jnp.float32),
            pltpu.VMEM((top, rows, lanes), jnp.float32),
            pltpu.VMEM((planes, rows, lanes), jnp.float32),
            pltpu.VMEM((top, rows, lanes), jnp.float32),
        ],
        compiler_params=pltpu.CompilerParams(vmem_limit_bytes=40 * 1024 * 1024),
    )(field, *pots, low, high, *seams)


def inner_pairs(step):
    half = SIDE * SIDE
    seam = half - 1 if step == 1 else 0
    return [(i, i + step) for i in range(2 * half) if i % half != seam]


def seam_pairs():
    half = SIDE * SIDE
    pairs = []
    for h in (0, 1):
        other = (1 - h) * half
        pairs += [(h * half + half - 1, other), (h * half, other + half - 1)]
    return pairs


def detour_pairs(route):
    half, last = SIDE * SIDE, SIDE - 1
    up, down = DETOURS[route] * SIDE + last, (last - DETOURS[route]) * SIDE
    out, back = [], []
    for h in (0, 1):
        own, other = h * half, (1 - h) * half
        out += [(own + half - 1, own + up), (own, own + down)]
        back += [(own + up, other), (own + down, other + half - 1)]
    return out, back


def halos(field, pot):
    planes = field.shape[1]
    at = lax.rem(lax.axis_index("domain"), SIDE * SIDE)

    def across(first, stop):
        block = field[first:stop]
        return jnp.where(at == 0, block[:, :DEPTH], block[:, planes - DEPTH :])

    blocks, first = [], 0
    for share in SHARES:
        blocks.append(across(first, first + share))
        first += share
    last = jnp.where(at == 0, pot[:DEPTH], pot[planes - DEPTH :])
    blocks[0] = jnp.concatenate([blocks[0], last[None]])
    seams = [lax.ppermute(blocks[0], "domain", seam_pairs())]
    for route, block in enumerate(blocks[1:]):
        out, back = detour_pairs(route)
        seams.append(lax.ppermute(lax.ppermute(block, "domain", out), "domain", back))
    field, pot, *_ = lax.optimization_barrier((field, pot, *blocks))
    both = jnp.concatenate([field, pot[None]])
    low = lax.ppermute(both[:, planes - DEPTH :], "domain", inner_pairs(1))
    high = lax.ppermute(both[:, :DEPTH], "domain", inner_pairs(-1))
    return low, high, seams


def thirds(block):
    first = block.astype(jnp.bfloat16)
    rest = block - first.astype(jnp.float32)
    second = rest.astype(jnp.bfloat16)
    return first, second, (rest - second.astype(jnp.float32)).astype(jnp.bfloat16)


def gram_kernel(pieces, cells, *rest):
    refs, (flat, own, other, gram) = rest[:-4], rest[-4:]
    me = lax.axis_index("band")
    lanes = refs[0].shape[1]
    share = refs[0].shape[0] // cells
    for index, ref in enumerate(refs):
        slot, piece = divmod(index, pieces)
        first = jnp.bitwise_xor(me, slot) * (share * pieces) + piece * share
        rows = pl.ds(pl.multiple_of(first, share), share)
        for r in range(cells):
            flat[rows, r * lanes : (r + 1) * lanes] = ref[pl.ds(r, share, stride=cells), :]
    one, two, three = thirds(flat[...])
    size = flat.shape[0]

    def product(left, right):
        return lax.dot_general(
            left, right, (((1,), (1,)), ((), ())), preferred_element_type=jnp.float32
        )

    wide = product(one, jnp.concatenate([one, two]))
    cross = wide[:, size:] + product(one, three)
    gram[...] = wide[:, :size] + (product(two, two) + (cross + cross.T))
    half = gram.shape[0] // 2
    core = lax.rem(lax.axis_index("band"), 2)
    own[...] = gram[pl.ds(pl.multiple_of(core * half, half), half)]
    other[...] = gram[pl.ds(pl.multiple_of((1 - core) * half, half), half)]


def flat_and_gram(slots, orbitals):
    pieces = len(slots[0])
    _, planes, width, lanes = slots[0][0].shape
    cells = planes * width
    refs = [piece.reshape(-1, lanes) for slot in slots for piece in slot]
    return pl.pallas_call(
        functools.partial(gram_kernel, pieces, cells),
        out_shape=[
            jax.ShapeDtypeStruct((orbitals, cells * lanes), jnp.float32),
            jax.ShapeDtypeStruct((orbitals // 2, orbitals), jnp.float32),
            jax.ShapeDtypeStruct((orbitals // 2, orbitals), jnp.float32),
        ],
        scratch_shapes=[pltpu.VMEM((orbitals, orbitals), jnp.float32)],
        compiler_params=pltpu.CompilerParams(vmem_limit_bytes=32 * 1024 * 1024),
    )(*refs)


def factor_kernel(panel, scale, own, other, out, left, right):
    half, orbitals = own.shape
    core = lax.rem(lax.axis_index("band"), 2)
    row = lax.broadcasted_iota(jnp.int32, (orbitals, orbitals), 0)
    lane = lax.broadcasted_iota(jnp.int32, (orbitals, orbitals), 1)
    left[pl.ds(pl.multiple_of(core * half, half), half)] = own[...]
    left[pl.ds(pl.multiple_of((1 - core) * half, half), half)] = other[...]
    right[...] = jnp.where(row == lane, scale, 0.0)
    inner = lax.broadcasted_iota(jnp.int32, (panel, orbitals), 0)
    for start in range(0, orbitals, panel):
        stop = start + panel
        rows_left = left[start:stop]
        rows_right = right[start:stop]
        columns = [
            jnp.broadcast_to(rows_left[:, start + k : start + k + 1], (panel, orbitals))
            for k in range(panel)
        ]
        roots = jnp.zeros((panel, orbitals), jnp.float32)
        for j in range(panel):
            pivot = jnp.broadcast_to(columns[j][j : j + 1], (panel, orbitals))
            roots = jnp.where(inner == j, lax.rsqrt(pivot), roots)
            if j == panel - 1:
                break
            factor = jnp.where(inner > j, columns[j] / pivot, 0.0)
            for k in range(j + 1, panel):
                columns[k] = columns[k] - factor * columns[k][j : j + 1]
            rows_left = rows_left - factor * rows_left[j : j + 1]
            rows_right = rows_right - factor * rows_right[j : j + 1]
        rows_left = rows_left * roots
        rows_right = rows_right * roots
        out[start:stop] = rows_right
        if stop < orbitals:
            for ref, rows in ((left, rows_left), (right, rows_right)):
                update = lax.dot_general(
                    rows_left,
                    rows,
                    (((0,), (0,)), ((), ())),
                    precision=lax.Precision.HIGHEST,
                    preferred_element_type=jnp.float32,
                )
                ref[stop:] = ref[stop:] - update[stop:]


def scaled_inverse(own, other, scale):
    orbitals = own.shape[1]
    return pl.pallas_call(
        functools.partial(factor_kernel, PANEL, scale),
        out_shape=jax.ShapeDtypeStruct((orbitals, orbitals), jnp.float32),
        scratch_shapes=[pltpu.VMEM((orbitals, orbitals), jnp.float32)] * 2,
        compiler_params=pltpu.CompilerParams(vmem_limit_bytes=32 * 1024 * 1024),
    )(own, other)


def rotate_kernel(inverse, flat, out):
    width, lanes = out.shape[2:]
    a, b = thirds(inverse[...]), thirds(flat[...])

    def product(left, right):
        left = jnp.concatenate([a[left[0]], a[left[1]]], axis=1)
        right = jnp.concatenate([b[right[0]], b[right[1]]])
        return jnp.dot(left, right, preferred_element_type=jnp.float32)

    small = product((1, 2), (1, 0)) + product((0, 0), (2, 1))
    solved = product((0, 1), (0, 0)) + small
    for r in range(width):
        out[:, 0, r, :] = solved[:, r * lanes : (r + 1) * lanes]


def rotated(inverse, flat, planes, lanes):
    orbitals, columns = flat.shape
    block = columns // planes
    shape = (orbitals, planes, block // lanes, lanes)
    return pl.pallas_call(
        rotate_kernel,
        grid=(planes,),
        in_specs=[
            pl.BlockSpec((orbitals, orbitals), lambda i: (0, 0)),
            pl.BlockSpec((orbitals, block), lambda i: (0, i)),
        ],
        out_specs=pl.BlockSpec((orbitals, 1, *shape[2:]), lambda i: (0, i, 0, 0)),
        out_shape=jax.ShapeDtypeStruct(shape, jnp.float32),
        compiler_params=pltpu.CompilerParams(vmem_limit_bytes=32 * 1024 * 1024),
    )(inverse, flat)


def summed(own, other):
    bands, half = lax.axis_size("band"), SIDE * SIDE
    depth = lax.axis_size("domain") // half * bands // 2

    def along_z(block, step):
        pairs = []
        for domain in range(lax.axis_size("domain")):
            for band in range(bands):
                z = (domain // half * (bands // 2) + band // 2 + step) % depth
                there = z // (bands // 2) * half + domain % half
                pairs.append((domain * bands + band, there * bands + z % (bands // 2) * 2 + band % 2))
        return lax.ppermute(block, ("domain", "band"), pairs)

    def turned(block, target):
        parts = [permuted(block, "domain", lambda i: target(i, k)) for k in (1, 2, 3)]
        return (block + parts[0]) + (parts[1] + parts[2])

    own = own + permuted(other, "band", lambda i: i ^ 1)
    own = own + permuted(own, "band", lambda i: i ^ 2)
    parts = [along_z(own, step) for step in (2, -2, 4)]
    own = (own + parts[2]) + (parts[0] + parts[1])
    own = turned(own, lambda i, k: i // SIDE * SIDE + (i + k) % SIDE)
    own = turned(own, lambda i, k: i // half * half + (i + k * SIDE) % half)
    return own, permuted(own, "band", lambda i: i ^ 1)


def body(orbitals, potential):
    stripes = lax.axis_size("band")
    own, planes, ny_all, nx_all = orbitals.shape
    orb_total = own * stripes
    cell_total = planes * lax.axis_size("domain") * ny_all * nx_all

    cut = SHARES[0]
    low, high, (seam, *others) = halos(orbitals, potential)
    pots = (potential, low[own], high[own], seam[cut])

    def sent(slots, chosen):
        return [permuted(slots[k], "band", lambda i: i ^ k) for k in chosen]

    slots = filtered_stripes(orbitals[:cut], pots, low, high, 0, [seam], stripes)
    early = sent(slots, EARLY)
    count = len(others)
    if TIED:
        tied = lax.optimization_barrier((*others, *early))
        others, early = tied[:count], list(tied[count:])
    rest = [k for k in range(1, stripes) if k not in EARLY]
    first = dict(zip([0, *EARLY, *rest], [slots[0], *early, *sent(slots, rest)]))
    slots = filtered_stripes(orbitals[cut:], pots, low, high, cut, others, stripes)
    second = [slots[0], *sent(slots, range(1, stripes))]
    slots = [[first[k], second[k]] for k in range(stripes)]
    flat, own_half, other_half = flat_and_gram(slots, orb_total)
    inverse = scaled_inverse(*summed(own_half, other_half), math.sqrt(cell_total))
    return rotated(inverse, flat, planes, nx_all)


def solution(mesh):
    in_specs = (P("band", "domain", None, None), P("domain", None, None))
    out_specs = P(None, "domain", "band", None)
    return jax.shard_map(body, mesh=mesh, in_specs=in_specs, out_specs=out_specs, check_vma=False)
```

```python
import functools
import math

import jax
import jax.numpy as jnp
from jax import lax
from jax.experimental import pallas as pl
from jax.experimental.pallas import tpu as pltpu
from jax.sharding import PartitionSpec as P

DEPTH = 3
TIED = True
EARLY = (1,)
PANEL = 32
SIDE = 4
SHARES = (8, 4, 4)
DETOURS = (0, 2)


def permuted(block, axis, target):
    count = lax.axis_size(axis)
    return lax.ppermute(block, axis, [(i, target(i)) for i in range(count)])


def neighbours(plane):
    rows, lanes = plane.shape
    beside = pltpu.roll(plane, 1, 0) + pltpu.roll(plane, rows - 1, 0)
    return beside + pltpu.roll(plane, 1, 1) + pltpu.roll(plane, lanes - 1, 1)


def filter_kernel(begin, shares, stripes, field, pot, pot_low, pot_high, pot_seam, low, high, *rest):
    routes = len(shares)
    seams, outs = rest[:routes], rest[routes : routes + stripes]
    zero, one, two, three, local = rest[routes + stripes :]
    me = lax.axis_index("band")
    at = lax.rem(lax.axis_index("domain"), SIDE * SIDE)
    at_low, at_high = at == 0, at == SIDE * SIDE - 1
    planes = field.shape[1]
    top = planes + 2 * DEPTH
    width = outs[0].shape[2]
    own = pl.ds(DEPTH, planes)
    local[own] = 0.8 * pot[...] - 1.2
    local[:DEPTH] = 0.8 * jnp.where(at_low, pot_seam[...], pot_low[...]) - 1.2
    local[planes + DEPTH :] = 0.8 * jnp.where(at_high, pot_seam[...], pot_high[...]) - 1.2

    def one_orbital(orbital, seam_plane):
        zero[own] = field[orbital]
        for k in range(DEPTH):
            zero[k] = jnp.where(at_low, seam_plane(k), low[begin + orbital, k])
            zero[planes + DEPTH + k] = jnp.where(at_high, seam_plane(k), high[begin + orbital, k])
        for k in range(1, top - 1):
            beside = zero[k - 1] + zero[k + 1] + neighbours(zero[k])
            one[k] = (0.5 * local[k]) * zero[k] - 0.2 * beside
        for k in range(2, top - 2):
            beside = one[k - 1] + one[k + 1] + neighbours(one[k])
            two[k] = local[k] * one[k] - 0.4 * beside - zero[k]
        for k in range(3, top - 3):
            beside = two[k - 1] + two[k + 1] + neighbours(two[k])
            three[k - 3] = local[k] * two[k] - 0.4 * beside - one[k]
        for slot in range(stripes):
            start = pl.multiple_of(jnp.bitwise_xor(me, slot) * width, width)
            outs[slot][orbital] = three[:, pl.ds(start, width), :]

    first = 0
    for share, seam in zip(shares, seams):

        def step(i, carry, first=first, seam=seam):
            one_orbital(first + i, lambda k: seam[i, k])
            return carry

        lax.fori_loop(0, share, step, 0)
        first += share


def filtered_stripes(field, pots, low, high, begin, seams, stripes):
    count, planes, rows, lanes = field.shape
    width = rows // stripes
    top = planes + 2 * DEPTH
    shares = [min(seam.shape[0], count) for seam in seams]
    shape = jax.ShapeDtypeStruct((count, planes, width, lanes), jnp.float32)
    return pl.pallas_call(
        functools.partial(filter_kernel, begin, shares, stripes),
        out_shape=[shape] * stripes,
        scratch_shapes=[
            pltpu.VMEM((top, rows, lanes), jnp.float32),
            pltpu.VMEM((top, rows, lanes), jnp.float32),
            pltpu.VMEM((top, rows, lanes), jnp.float32),
            pltpu.VMEM((planes, rows, lanes), jnp.float32),
            pltpu.VMEM((top, rows, lanes), jnp.float32),
        ],
        compiler_params=pltpu.CompilerParams(vmem_limit_bytes=40 * 1024 * 1024),
    )(field, *pots, low, high, *seams)


def inner_pairs(step):
    half = SIDE * SIDE
    seam = half - 1 if step == 1 else 0
    return [(i, i + step) for i in range(2 * half) if i % half != seam]


def seam_pairs():
    half = SIDE * SIDE
    pairs = []
    for h in (0, 1):
        other = (1 - h) * half
        pairs += [(h * half + half - 1, other), (h * half, other + half - 1)]
    return pairs


def detour_pairs(route):
    half, last = SIDE * SIDE, SIDE - 1
    up, down = DETOURS[route] * SIDE + last, (last - DETOURS[route]) * SIDE
    out, back = [], []
    for h in (0, 1):
        own, other = h * half, (1 - h) * half
        out += [(own + half - 1, own + up), (own, own + down)]
        back += [(own + up, other), (own + down, other + half - 1)]
    return out, back


def halos(field, pot):
    planes = field.shape[1]
    at = lax.rem(lax.axis_index("domain"), SIDE * SIDE)

    def across(first, stop):
        block = field[first:stop]
        return jnp.where(at == 0, block[:, :DEPTH], block[:, planes - DEPTH :])

    blocks, first = [], 0
    for share in SHARES:
        blocks.append(across(first, first + share))
        first += share
    last = jnp.where(at == 0, pot[:DEPTH], pot[planes - DEPTH :])
    blocks[0] = jnp.concatenate([blocks[0], last[None]])
    seams = [lax.ppermute(blocks[0], "domain", seam_pairs())]
    for route, block in enumerate(blocks[1:]):
        out, back = detour_pairs(route)
        seams.append(lax.ppermute(lax.ppermute(block, "domain", out), "domain", back))
    field, pot, *_ = lax.optimization_barrier((field, pot, *blocks))
    both = jnp.concatenate([field, pot[None]])
    low = lax.ppermute(both[:, planes - DEPTH :], "domain", inner_pairs(1))
    high = lax.ppermute(both[:, :DEPTH], "domain", inner_pairs(-1))
    return low, high, seams


def thirds(block):
    first = block.astype(jnp.bfloat16)
    rest = block - first.astype(jnp.float32)
    second = rest.astype(jnp.bfloat16)
    return first, second, (rest - second.astype(jnp.float32)).astype(jnp.bfloat16)


def gram_kernel(pieces, cells, *rest):
    refs, (flat, own, other, gram) = rest[:-4], rest[-4:]
    me = lax.axis_index("band")
    lanes = refs[0].shape[1]
    share = refs[0].shape[0] // cells
    for index, ref in enumerate(refs):
        slot, piece = divmod(index, pieces)
        first = jnp.bitwise_xor(me, slot) * (share * pieces) + piece * share
        rows = pl.ds(pl.multiple_of(first, share), share)
        for r in range(cells):
            flat[rows, r * lanes : (r + 1) * lanes] = ref[pl.ds(r, share, stride=cells), :]
    one, two, three = thirds(flat[...])
    size = flat.shape[0]

    def product(left, right):
        return lax.dot_general(
            left, right, (((1,), (1,)), ((), ())), preferred_element_type=jnp.float32
        )

    wide = product(one, jnp.concatenate([one, two]))
    cross = wide[:, size:] + product(one, three)
    gram[...] = wide[:, :size] + (product(two, two) + (cross + cross.T))
    half = gram.shape[0] // 2
    core = lax.rem(lax.axis_index("band"), 2)
    own[...] = gram[pl.ds(pl.multiple_of(core * half, half), half)]
    other[...] = gram[pl.ds(pl.multiple_of((1 - core) * half, half), half)]


def flat_and_gram(slots, orbitals):
    pieces = len(slots[0])
    _, planes, width, lanes = slots[0][0].shape
    cells = planes * width
    refs = [piece.reshape(-1, lanes) for slot in slots for piece in slot]
    return pl.pallas_call(
        functools.partial(gram_kernel, pieces, cells),
        out_shape=[
            jax.ShapeDtypeStruct((orbitals, cells * lanes), jnp.float32),
            jax.ShapeDtypeStruct((orbitals // 2, orbitals), jnp.float32),
            jax.ShapeDtypeStruct((orbitals // 2, orbitals), jnp.float32),
        ],
        scratch_shapes=[pltpu.VMEM((orbitals, orbitals), jnp.float32)],
        compiler_params=pltpu.CompilerParams(vmem_limit_bytes=32 * 1024 * 1024),
    )(*refs)


def factor_kernel(panel, scale, own, other, out, left, right):
    half, orbitals = own.shape
    core = lax.rem(lax.axis_index("band"), 2)
    row = lax.broadcasted_iota(jnp.int32, (orbitals, orbitals), 0)
    lane = lax.broadcasted_iota(jnp.int32, (orbitals, orbitals), 1)
    left[pl.ds(pl.multiple_of(core * half, half), half)] = own[...]
    left[pl.ds(pl.multiple_of((1 - core) * half, half), half)] = other[...]
    right[...] = jnp.where(row == lane, scale, 0.0)
    inner = lax.broadcasted_iota(jnp.int32, (panel, orbitals), 0)
    for start in range(0, orbitals, panel):
        stop = start + panel
        rows_left = left[start:stop]
        rows_right = right[start:stop]
        columns = [
            jnp.broadcast_to(rows_left[:, start + k : start + k + 1], (panel, orbitals))
            for k in range(panel)
        ]
        roots = jnp.zeros((panel, orbitals), jnp.float32)
        for j in range(panel):
            pivot = jnp.broadcast_to(columns[j][j : j + 1], (panel, orbitals))
            roots = jnp.where(inner == j, lax.rsqrt(pivot), roots)
            if j == panel - 1:
                break
            factor = jnp.where(inner > j, columns[j] / pivot, 0.0)
            for k in range(j + 1, panel):
                columns[k] = columns[k] - factor * columns[k][j : j + 1]
            rows_left = rows_left - factor * rows_left[j : j + 1]
            rows_right = rows_right - factor * rows_right[j : j + 1]
        rows_left = rows_left * roots
        rows_right = rows_right * roots
        out[start:stop] = rows_right
        if stop < orbitals:
            for ref, rows in ((left, rows_left), (right, rows_right)):
                update = lax.dot_general(
                    rows_left,
                    rows,
                    (((0,), (0,)), ((), ())),
                    precision=lax.Precision.HIGHEST,
                    preferred_element_type=jnp.float32,
                )
                ref[stop:] = ref[stop:] - update[stop:]


def scaled_inverse(own, other, scale):
    orbitals = own.shape[1]
    return pl.pallas_call(
        functools.partial(factor_kernel, PANEL, scale),
        out_shape=jax.ShapeDtypeStruct((orbitals, orbitals), jnp.float32),
        scratch_shapes=[pltpu.VMEM((orbitals, orbitals), jnp.float32)] * 2,
        compiler_params=pltpu.CompilerParams(vmem_limit_bytes=32 * 1024 * 1024),
    )(own, other)


def rotate_kernel(inverse, flat, out):
    width, lanes = out.shape[2:]
    a, b = thirds(inverse[...]), thirds(flat[...])

    def product(left, right):
        left = jnp.concatenate([a[left[0]], a[left[1]]], axis=1)
        right = jnp.concatenate([b[right[0]], b[right[1]]])
        return jnp.dot(left, right, preferred_element_type=jnp.float32)

    small = product((1, 2), (1, 0)) + product((0, 0), (2, 1))
    solved = product((0, 1), (0, 0)) + small
    for r in range(width):
        out[:, 0, r, :] = solved[:, r * lanes : (r + 1) * lanes]


def rotated(inverse, flat, planes, lanes):
    orbitals, columns = flat.shape
    block = columns // planes
    shape = (orbitals, planes, block // lanes, lanes)
    return pl.pallas_call(
        rotate_kernel,
        grid=(planes,),
        in_specs=[
            pl.BlockSpec((orbitals, orbitals), lambda i: (0, 0)),
            pl.BlockSpec((orbitals, block), lambda i: (0, i)),
        ],
        out_specs=pl.BlockSpec((orbitals, 1, *shape[2:]), lambda i: (0, i, 0, 0)),
        out_shape=jax.ShapeDtypeStruct(shape, jnp.float32),
        compiler_params=pltpu.CompilerParams(vmem_limit_bytes=32 * 1024 * 1024),
    )(inverse, flat)


def summed(own, other):
    bands, half = lax.axis_size("band"), SIDE * SIDE
    depth = lax.axis_size("domain") // half * bands // 2

    def along_z(block, step):
        pairs = []
        for domain in range(lax.axis_size("domain")):
            for band in range(bands):
                z = (domain // half * (bands // 2) + band // 2 + step) % depth
                there = z // (bands // 2) * half + domain % half
                pairs.append((domain * bands + band, there * bands + z % (bands // 2) * 2 + band % 2))
        return lax.ppermute(block, ("domain", "band"), pairs)

    def turned(block, target):
        parts = [permuted(block, "domain", lambda i: target(i, k)) for k in (1, 2, 3)]
        return (block + parts[0]) + (parts[1] + parts[2])

    own = own + permuted(other, "band", lambda i: i ^ 1)
    own = own + permuted(own, "band", lambda i: i ^ 2)
    parts = [along_z(own, step) for step in (2, -2, 4)]
    own = (own + parts[2]) + (parts[0] + parts[1])
    own = turned(own, lambda i, k: i // SIDE * SIDE + (i + k) % SIDE)
    own = turned(own, lambda i, k: i // half * half + (i + k * SIDE) % half)
    return own, permuted(own, "band", lambda i: i ^ 1)


def body(orbitals, potential):
    stripes = lax.axis_size("band")
    own, planes, ny_all, nx_all = orbitals.shape
    orb_total = own * stripes
    cell_total = planes * lax.axis_size("domain") * ny_all * nx_all

    cut = SHARES[0]
    low, high, (seam, *others) = halos(orbitals, potential)
    pots = (potential, low[own], high[own], seam[cut])

    def sent(slots, chosen):
        return [permuted(slots[k], "band", lambda i: i ^ k) for k in chosen]

    slots = filtered_stripes(orbitals[:cut], pots, low, high, 0, [seam], stripes)
    early = sent(slots, EARLY)
    count = len(others)
    if TIED:
        tied = lax.optimization_barrier((*others, *early))
        others, early = tied[:count], list(tied[count:])
    rest = [k for k in range(1, stripes) if k not in EARLY]
    first = dict(zip([0, *EARLY, *rest], [slots[0], *early, *sent(slots, rest)]))
    slots = filtered_stripes(orbitals[cut:], pots, low, high, cut, others, stripes)
    second = [slots[0], *sent(slots, range(1, stripes))]
    slots = [[first[k], second[k]] for k in range(stripes)]
    flat, own_half, other_half = flat_and_gram(slots, orb_total)
    inverse = scaled_inverse(*summed(own_half, other_half), math.sqrt(cell_total))
    return rotated(inverse, flat, planes, nx_all)


def solution(mesh):
    in_specs = (P("band", "domain", None, None), P("domain", None, None))
    out_specs = P(None, "domain", "band", None)
    return jax.shard_map(body, mesh=mesh, in_specs=in_specs, out_specs=out_specs, check_vma=False)
```
